32 devices in a mesh: seq: 4 (over y, x), fsdp: 8 (over z, core).
Axes of the slice: x: 2, y: 2, z: 4, core: 2. Of those that a mesh axis runs over, the one named last changes fastest.
Arguments:
- tokens: bfloat16 [8, 1536, 1536], P('fsdp', 'seq'), may hold values from -6 to 6
- cotangent: bfloat16 [8, 1536, 1536], P('fsdp', 'seq'), may hold values from -6 to 6
- prefix_len: int32 [8], P('fsdp'), may hold values from 153 to 768
- expert_ids: int32 [8, 1536, 8], P('fsdp', 'seq'), may hold values from 0 to 15, all different within a row
- slot_rank: int32 [8, 4, 3072], P('fsdp', 'seq'), may hold values from 0 to 3071, each once within a row
- norm1_gain: bfloat16 [2, 1536], P(None, ('seq', 'fsdp')), may hold values from 0.5 to 1.5
- qkv_weight: bfloat16 [2, 1536, 2560], P(None, ('seq', 'fsdp')), may hold values from -0.15625 to 0.15625
- out_weight: bfloat16 [2, 1536, 1536], P(None, ('seq', 'fsdp')), may hold values from -1.25 to 1.25
- norm2_gain: bfloat16 [2, 1536], P(None, ('seq', 'fsdp')), may hold values from 0.5 to 1.5
- router_weight: bfloat16 [2, 1536, 16], P(None, ('seq', 'fsdp')), may hold values from -0.078125 to 0.078125
- in_weight: bfloat16 [2, 1536, 16384], P(None, 'seq', 'fsdp'), may hold values from -0.15625 to 0.15625
- down_weight: bfloat16 [2, 1536, 8192], P(None, 'seq', 'fsdp'), may hold values from -1 to 1
Outputs:
- output: bfloat16 [8, 1536, 1536], P('fsdp', 'seq')
- input_grad: float32 [8, 1536, 1536], P('fsdp', 'seq')
- norm1_grad: float32 [2, 1536], P(None, ('seq', 'fsdp'))
- qkv_grad: float32 [2, 1536, 2560], P(None, ('seq', 'fsdp'))
- out_grad: float32 [2, 1536, 1536], P(None, ('seq', 'fsdp'))
- norm2_grad: float32 [2, 1536], P(None, ('seq', 'fsdp'))
- router_grad: float32 [2, 1536, 16], P(None, ('seq', 'fsdp'))
- in_grad: float32 [2, 1536, 16384], P(None, 'seq', 'fsdp')
- down_grad: float32 [2, 1536, 8192], P(None, 'seq', 'fsdp')
The draws below stay inside these ranges and needn't reach their ends.
Inputs may be any that keep to these rules, and one draw needn't show every extreme that they name: `expert_ids`: each token names 8 different experts. `slot_rank`: for each sequence and piece, a permutation of 0 to 3071.
All inputs are finite; a program needn't handle non-finite values.
Results may differ from the reference program's by a relative error of at most 0.025.
Values may be sent and summed in bfloat16 or wider, within the bound.
No kernel may reach another device: no remote copies, remote signals or barrier semaphores. Data moves between devices by JAX's collectives and lax.ppermute only.
A program may use at most 832 MiB of HBM per device.

```python
import jax
import jax.numpy as jnp
from jax import lax

D = 1536
HEADS = 24
KV_HEADS = 8
HEAD_DIM = 64
FF = 512
TOP = 8
EXPERTS = 16
LAYERS = 2
SEQ_LEN = 1536
SEQS = 8
PIECE = 384
CAPACITY = 240
Q_WIDTH = 1536
QKV_WIDTH = 2560
N_SEQ = 4


def place_ends(drawn, stream_key, low, largest):
    index_at = [jax.random.randint(jax.random.fold_in(stream_key, axis), (), 0, length) for axis, length in enumerate(drawn.shape)]
    widest = drawn.shape.index(max(drawn.shape))
    next_to = index_at[:widest] + [(index_at[widest] + 1) % drawn.shape[widest]] + index_at[widest + 1:]
    return drawn.at[tuple(index_at)].set(low).at[tuple(next_to)].set(largest)


def block_scale(stream_key, dims, cuts, least, top_value):
    def one(axis_at, blocks):
        heights = jax.random.uniform(jax.random.fold_in(jax.random.fold_in(stream_key, 6), axis_at), (blocks,), jnp.float32, least / len(cuts), top_value / len(cuts))
        return jnp.repeat(jnp.exp(heights), dims[axis_at] // blocks).reshape((-1,) + (1,) * (len(dims) - axis_at - 1))

    loudness = one(*cuts[0])
    for cut in cuts[1:]:
        loudness = loudness * one(*cut)
    return loudness


def choose_distinct(stream_key, rows, count, top, lift):
    ranking = jax.random.permutation(jax.random.fold_in(stream_key, 1), count)
    boost = ranking
    for power in range(3):
        boost = boost * boost // count
    boost = boost * lift // count
    lots = jax.random.randint(jax.random.fold_in(stream_key, 2), (rows, count), 0, 4096) + boost
    holders = jax.random.permutation(jax.random.fold_in(stream_key, 3), rows)[jnp.arange(count) % rows]
    lots = jnp.where(jnp.arange(rows)[:, None] == holders[None, :], 1 << 14, lots)
    score = lots * count + jnp.arange(count)
    return lax.top_k(score.astype(jnp.int32), top)[1].astype(jnp.int32)


def gaussian(own_key, extent, width, bound, split=(), held_as=jnp.bfloat16):
    drawn = width * jax.random.normal(own_key, extent, jnp.float32)
    if split:
        drawn = drawn * block_scale(own_key, extent, split, -0.22, 0.18)
    return jnp.clip(drawn, -bound, bound).astype(held_as)


def setup_inputs(seed: int = 0) -> dict:
    key_of = jax.random.split(jax.random.key(seed), 13)
    return {
        "tokens": gaussian(key_of[0], (SEQS, SEQ_LEN, D), 1.0, 6.0, ((0, 8), (1, 4))),
        "cotangent": gaussian(key_of[1], (SEQS, SEQ_LEN, D), 1.0, 6.0, ((0, 8), (1, 4))),
        "prefix_len": place_ends(jax.random.randint(key_of[2], (SEQS,), SEQ_LEN // 10, SEQ_LEN // 2 + 1), jax.random.fold_in(key_of[2], 1), SEQ_LEN // 10, (SEQ_LEN // 2 + 1) - 1).astype(jnp.int32),
        "expert_ids": choose_distinct(key_of[3], SEQS * SEQ_LEN, EXPERTS, TOP, 4096).reshape((SEQS, SEQ_LEN, TOP)),
        "slot_rank": jax.vmap(lambda own: jax.random.permutation(own, PIECE * TOP))(jax.random.split(key_of[4], SEQS * N_SEQ)).reshape((SEQS, N_SEQ, PIECE * TOP)).astype(jnp.int32),
        "norm1_gain": jnp.clip(1.0 + 0.1 * jax.random.normal(key_of[5], (LAYERS, D), jnp.float32), 0.5, 1.5).astype(jnp.bfloat16),
        "qkv_weight": gaussian(key_of[6], (LAYERS, D, QKV_WIDTH), D ** -0.5, 0.15625, ((1, 32),)),
        "out_weight": gaussian(key_of[7], (LAYERS, D, Q_WIDTH), (max(Q_WIDTH // 64, 1)) ** -0.5, 1.25, ((1, 32),)),
        "norm2_gain": jnp.clip(1.0 + 0.1 * jax.random.normal(key_of[8], (LAYERS, D), jnp.float32), 0.5, 1.5).astype(jnp.bfloat16),
        "router_weight": gaussian(key_of[9], (LAYERS, D, EXPERTS), (4 * D) ** -0.5, 0.078125, ((1, 32),)),
        "in_weight": gaussian(key_of[10], (LAYERS, D, EXPERTS * 2 * FF), D ** -0.5, 0.15625, ((1, 4), (2, 8))),
        "down_weight": gaussian(key_of[11], (LAYERS, D, EXPERTS * FF), (FF // 16) ** -0.5, 1.0, ((1, 4), (2, 8))),
    }


EPS = 1e-06
THETA = 10000.0
SCALE = 0.125
HIGH = lax.Precision.HIGHEST

@jax.custom_vjp
def low(v):
    return lax.optimization_barrier(v.astype(jnp.bfloat16)).astype(jnp.float32)

@jax.custom_vjp
def low_back(v):
    return v

def low_keep(v):
    return (low(v), None)

def low_pass(kept, grad):
    return (grad,)

def back_keep(v):
    return (v, None)

def back_low(kept, grad):
    return (low(grad),)
low.defvjp(low_keep, low_pass)
low_back.defvjp(back_keep, back_low)

def product(left, right):
    return jnp.dot(left, right, precision=HIGH)

def normalize(stream, gain):
    hat = stream * lax.rsqrt(lax.optimization_barrier(jnp.mean(stream * stream, axis=-1, keepdims=True)) + EPS)
    return low(hat * gain)

def turn(values):
    half = values.shape[-1] // 2
    return jnp.concatenate([-values[..., half:], values[..., :half]], axis=-1)

def tables(positions):
    steps = jnp.arange(HEAD_DIM // 2, dtype=jnp.float32)
    freqs = THETA ** (-2.0 * steps / HEAD_DIM)
    angles = positions.astype(jnp.float32)[:, None] * freqs[None, :]
    angles = jnp.concatenate([angles, angles], axis=-1)
    return (jnp.cos(angles), jnp.sin(angles))

def rotate(values, cosine, sine):
    return values * cosine[:, None, :] + turn(values) * sine[:, None, :]

def attend(query, keys, values, prefix_one):
    length = query.shape[0]
    block_len = min(512, length)
    block_count = length // block_len
    blocks = query.reshape(block_count, block_len, KV_HEADS, HEADS // KV_HEADS, HEAD_DIM)
    key_pos = jnp.arange(length, dtype=jnp.int32)

    def one_block(item):
        rows, first_row = item
        query_pos = first_row + jnp.arange(block_len, dtype=jnp.int32)
        scores = low_back(SCALE * jnp.einsum('qhgd,khd->hgqk', rows, keys, precision=HIGH))
        allowed = (key_pos[None, :] <= query_pos[:, None]) | (key_pos[None, :] < prefix_one)
        scores = jnp.where(allowed, scores, -jnp.inf)
        probs = low(jax.nn.softmax(scores, axis=-1))
        return jnp.einsum('hgqk,khd->qhgd', probs, values, precision=HIGH)
    firsts = jnp.arange(block_count, dtype=jnp.int32) * block_len
    result = lax.map(jax.checkpoint(one_block), (blocks, firsts))
    return result.reshape(length, HEADS * HEAD_DIM)

def routing(expert_ids, slot_rank):
    pairs = expert_ids.reshape(N_SEQ, PIECE * TOP)
    earlier = slot_rank[:, None, :] < slot_rank[:, :, None]
    same = pairs[:, None, :] == pairs[:, :, None]
    position = lax.optimization_barrier(jnp.sum((earlier & same).astype(jnp.int32), axis=-1))
    slot_ids = jnp.where(position < CAPACITY, pairs * CAPACITY + position, -1)
    return slot_ids.reshape(N_SEQ, PIECE, TOP)

def layer(stream, weights, prefix_one, expert_ids, slot_ids, cosine, sine):
    gain_one, w_qkv, w_out, gain_two, w_router, w_in, w_down = weights
    query_width = HEADS * HEAD_DIM
    key_width = KV_HEADS * HEAD_DIM
    length = stream.shape[0]
    normed = normalize(stream, gain_one)
    mixed = low_back(product(normed, w_qkv))
    query = mixed[:, :query_width].reshape(length, HEADS, HEAD_DIM)
    keys = mixed[:, query_width:query_width + key_width].reshape(length, KV_HEADS, HEAD_DIM)
    values = low(mixed[:, query_width + key_width:].reshape(length, KV_HEADS, HEAD_DIM))
    query = low_back(low(rotate(query, cosine, sine)))
    keys = low_back(low(rotate(keys, cosine, sine)))
    grouped = query.reshape(length, KV_HEADS, HEADS // KV_HEADS, HEAD_DIM)
    attended = low_back(low(attend(grouped, keys, values, prefix_one)))
    hidden = stream + low_back(jnp.dot(attended, w_out.T, precision=HIGH))
    normed_two = normalize(hidden, gain_two)
    logits = low_back(product(normed_two, w_router))
    ids_hot = (expert_ids[:, :, None] == jnp.arange(EXPERTS, dtype=jnp.int32)[None, None, :]).astype(jnp.float32)
    chosen = lax.optimization_barrier(jnp.sum(logits[:, None, :] * ids_hot, axis=-1))
    gates = jax.nn.softmax(chosen, axis=-1)
    columns = jnp.arange(EXPERTS * CAPACITY, dtype=jnp.int32)
    slot_hot = (slot_ids[..., None] == columns).astype(jnp.float32)
    dispatch = lax.optimization_barrier(jnp.sum(slot_hot, axis=2))
    combine = low(jnp.einsum('gtk,gtks->gts', gates.reshape(N_SEQ, PIECE, TOP), slot_hot, precision=HIGH))
    tokens_in = normed_two.reshape(N_SEQ, PIECE, D)
    sent = low_back(jnp.einsum('gts,gtd->gsd', dispatch, tokens_in, precision=HIGH))
    sent = sent.reshape(N_SEQ, EXPERTS, CAPACITY, D)
    both = low_back(jnp.einsum('gecd,def->gecf', sent, w_in.reshape(D, EXPERTS, 2 * FF), precision=HIGH))
    inner = low(jax.nn.silu(both[..., :FF]) * both[..., FF:])
    returned = jnp.einsum('gecf,def->gecd', inner, w_down.reshape(D, EXPERTS, FF), precision=HIGH)
    returned = low_back(low(returned)).reshape(N_SEQ, EXPERTS * CAPACITY, D)
    merged = low_back(jnp.einsum('gts,gsd->gtd', combine, returned, precision=HIGH))
    return hidden + merged.reshape(length, D)

def reference(tokens, cotangent, prefix_len, expert_ids, slot_rank, norm1_gain, qkv_weight, out_weight, norm2_gain, router_weight, in_weight, down_weight):
    weights = tuple((item.astype(jnp.float32) for item in (norm1_gain, qkv_weight, out_weight, norm2_gain, router_weight, in_weight, down_weight)))
    cosine, sine = tables(jnp.arange(SEQ_LEN, dtype=jnp.int32))

    def each_sequence(totals, item):
        stream, grad_out, prefix_one, ids_one, rank_one = item
        slot_ids = routing(ids_one, rank_one)

        def forward(values, params):
            for layer_index in range(LAYERS):
                values = layer(values, tuple((param[layer_index] for param in params)), prefix_one, ids_one, slot_ids, cosine, sine)
            return values
        result, pullback = jax.vjp(forward, stream.astype(jnp.float32), weights)
        grad_input, grads = pullback(grad_out.astype(jnp.float32))
        return (tuple((total + grad for total, grad in zip(totals, grads))), (result.astype(jnp.bfloat16), grad_input))
    zeros = tuple((jnp.zeros(item.shape, jnp.float32) for item in weights))
    totals, (outputs, grad_inputs) = lax.scan(each_sequence, zeros, (tokens, cotangent, prefix_len, expert_ids, slot_rank))
    return (outputs, grad_inputs, totals[0], totals[1], totals[2], totals[3], totals[4], totals[5], totals[6])
```

```python
import functools

import jax
import jax.numpy as jnp
from jax import lax
from jax.experimental import pallas as pl
from jax.experimental.pallas import tpu as pltpu
from jax.sharding import Mesh
from jax.sharding import PartitionSpec as P

HEADS = 24
KV_HEADS = 8
HEAD_DIM = 64
FF = 512
TOP = 8
EXPERTS = 16
LAYERS = 2
EPS = 1e-06
THETA = 10000.0
SCALE = 0.125
Q_WIDTH = HEADS * HEAD_DIM
K_WIDTH = KV_HEADS * HEAD_DIM
PAD = 128
SEQ_AXES = ("s1", "s0")
FSDP_AXES = ("fh", "fl", "c")
ALL_AXES = SEQ_AXES + FSDP_AXES
BF = jnp.bfloat16
F32 = jnp.float32


def normalize(values):
    factor = lax.rsqrt(jnp.mean(values * values, axis=-1, keepdims=True) + EPS)
    return (values * factor, factor)


def norm_back(grad_hat, hat_values, factor):
    inner = jnp.mean(grad_hat * hat_values, axis=-1, keepdims=True)
    return factor * (grad_hat - hat_values * inner)


def tables(positions):
    steps = jnp.arange(HEAD_DIM // 2, dtype=F32)
    freqs = THETA ** (-2.0 * steps / HEAD_DIM)
    angles = positions.astype(F32)[:, None] * freqs[None, :]
    cosine, sine = jnp.cos(angles), jnp.sin(angles)
    none = jnp.zeros_like(sine)
    return (
        jnp.concatenate([cosine, cosine], axis=-1),
        jnp.concatenate([-sine, none], axis=-1),
        jnp.concatenate([none, sine], axis=-1),
    )


def rotate(values, rotation, sign):
    cosine, ahead, behind = (
        jnp.tile(table, (1, values.shape[1] // HEAD_DIM)) for table in rotation
    )
    half = HEAD_DIM // 2
    later = jnp.roll(values, -half, axis=1)
    sooner = jnp.roll(values, half, axis=1)
    return values * cosine + sign * (later * ahead + sooner * behind)


def rounded(values):
    return lax.optimization_barrier(values.astype(BF)).astype(F32)


def swap(values, axis):
    return lax.ppermute(values, axis, [(0, 1), (1, 0)])


def tie(*values):
    return lax.optimization_barrier(values)


class Side:
    def __init__(self, steps):
        self.steps = steps
        self.pending = next(steps)
        self.result = None

    def advance(self, value):
        if self.result is not None:
            return
        try:
            self.pending = self.steps.send(value)
        except StopIteration as stop:
            self.pending, self.result = (), stop.value


def meet(sides, *values):
    pending, values = tie([side.pending for side in sides], values)
    for side, value in zip(sides, pending):
        side.advance(value)
    return values[0] if len(values) == 1 else values


def ring_start(values, axis):
    size = lax.axis_size(axis)
    blocks = []
    for step in range(1, size):
        values = lax.ppermute(values, axis, [(i, (i + 1) % size) for i in range(size)])
        blocks.append(values)
    return blocks


def in_order(blocks, axis):
    size = len(blocks)
    index = lax.axis_index(axis)
    if size == 2:
        first = index == 0
        return jnp.stack(
            [jnp.where(first, blocks[0], blocks[1]), jnp.where(first, blocks[1], blocks[0])]
        )
    result = jnp.zeros((size,) + blocks[0].shape, blocks[0].dtype)
    for step, block in enumerate(blocks):
        result = lax.dynamic_update_index_in_dim(result, block, (index - step) % size, 0)
    return result


def ring_gather(values, axis):
    return in_order([values] + ring_start(values, axis), axis)


def pick(blocks, index):
    return lax.dynamic_index_in_dim(blocks, index, 0, False)


def scatter_start(blocks, axis):
    size = lax.axis_size(axis)
    index = lax.axis_index(axis)
    carried = pick(blocks, (index + size - 1) % size)
    for step in range(1, size):
        carried = lax.ppermute(carried, axis, [(i, (i + 1) % size) for i in range(size)])
        if step < size - 1:
            mine = pick(blocks, (index + size - 1 - step) % size)
            carried = (carried.astype(F32) + mine.astype(F32)).astype(BF)
    return carried


def scatter_end(blocks, carried, axis):
    return carried.astype(F32) + pick(blocks, lax.axis_index(axis)).astype(F32)


def ring_scatter(blocks, axis):
    return scatter_end(blocks, scatter_start(blocks, axis), axis)


def high_end(part, received):
    rows, cols = part.shape
    high = lax.axis_size("fh")
    low_index = lax.axis_index("s0")
    if high == 2:
        same = lax.axis_index("fh") == low_index
        return (jnp.where(same, part, received[0]), jnp.where(same, received[0], part))
    blocks = in_order([part] + received, "fh").reshape(2, high // 2, rows, cols)
    join = lambda these: these.transpose(1, 0, 2).reshape(rows, high // 2 * cols)
    return (join(pick(blocks, low_index)), join(pick(blocks, 1 - low_index)))


def low_end(keep, received):
    rows, cols = keep.shape
    return in_order([keep, received], "s0").reshape(2 * rows, cols)


def rows_end(block, received):
    return in_order([block] + received, "s1").reshape(-1, block.shape[1])


def by_rows(full):
    return full.reshape(lax.axis_size("s1"), -1, full.shape[1])


def low_split(summed):
    high = lax.axis_size("fh")
    rows = summed.shape[0] // 2
    cols = summed.shape[1] // (high // 2)
    low_index = lax.axis_index("s0")
    halves = summed.reshape(2, rows, high // 2, cols).transpose(0, 2, 1, 3)
    return (pick(halves, low_index), pick(halves, 1 - low_index))


def all_high(keep, received):
    both = in_order([keep, received], "s0")
    return both.reshape((lax.axis_size("fh"),) + keep.shape[1:])


def on_chip_pairs(message, on_chip, sides):
    half = message.shape[0] // 2
    near = swap(message, "s0")
    low = swap(message, "fl")
    own = on_chip(message, swap(message, "c"))
    near, low, own = meet(sides, near, low, own)
    far_top = swap(low[:half], "s0")
    far_bottom = swap(near[half:], "fl")
    near_mate, low_mate = tie(swap(near, "c"), swap(low, "c"))
    near, low = tie(on_chip(near, near_mate), low)
    near_sum = swap(near[1], "c")
    own_sum = swap(own[1], "c")
    low = on_chip(low, low_mate)
    far_top, far_bottom, low, near_sum, own_sum = meet(
        sides, far_top, far_bottom, low, near_sum, own_sum
    )
    far = jnp.concatenate([far_top, far_bottom], axis=0)
    return (own, near, low, far, own_sum, near_sum)


def sums_home(own, near, low, far, own_sum, near_sum, on_chip, sides, late=None, last=None):
    half = far.shape[0] // 2
    far_mate = swap(far, "c")
    low_sum = swap(low[1], "c")
    near_sum = near[0].astype(F32) + near_sum.astype(F32)
    near_top = swap(near_sum[:half].astype(BF), "s0")
    far_mate, low_sum = tie(far_mate, low_sum)
    low_sum = low[0].astype(F32) + low_sum.astype(F32)
    low_bottom = swap(low_sum[half:].astype(BF), "fl")
    far = on_chip(far, far_mate)
    near_top, low_bottom, far = tie(near_top, low_bottom, far)
    far_sum = (far[0].astype(F32) + swap(far[1], "c").astype(F32)).astype(BF)
    kept = [own[2:], near[2:], low[2:], far[2:]]
    far_top = swap(far_sum[:half], "s0")
    far_bottom = swap(far_sum[half:], "fl")
    if late is not None:
        late = late(kept)
    far_top, far_bottom, late = tie(far_top, far_bottom, late)
    near_bottom = swap((near_sum[half:] + far_bottom.astype(F32)).astype(BF), "s0")
    low_top = swap((low_sum[:half] + far_top.astype(F32)).astype(BF), "fl")
    if last is not None:
        last = last(kept)
    near_bottom, low_top, last = meet(sides, near_bottom, low_top, last)
    own_sum = own[0].astype(F32) + own_sum.astype(F32)
    top = own_sum[:half] + near_top.astype(F32) + low_top.astype(F32)
    bottom = own_sum[half:] + near_bottom.astype(F32) + low_bottom.astype(F32)
    return (jnp.concatenate([top, bottom], axis=0), kept, late, last)


def through_experts(message, on_chip, sides, late=None, last=None):
    return sums_home(
        *on_chip_pairs(message, on_chip, sides), on_chip, sides, late=late, last=last
    )


def chip_sums_home(own, near, low, far):
    half = own[0].shape[0] // 2
    own, near, low, far = (
        pair[0].astype(F32) + swap(pair[1], "c").astype(F32) for pair in (own, near, low, far)
    )
    far = far.astype(BF)
    far_top = swap(far[:half], "s0").astype(F32)
    far_bottom = swap(far[half:], "fl").astype(F32)
    near = jnp.concatenate([near[:half], near[half:] + far_bottom], axis=0).astype(BF)
    low = jnp.concatenate([low[:half] + far_top, low[half:]], axis=0).astype(BF)
    return own + swap(near, "s0").astype(F32) + swap(low, "fl").astype(F32)


def sequence_gather(keys, values, sides):
    keys_near, values_near = ring_start(keys, "s0"), ring_start(values, "s1")
    keys_near, values_near = meet(sides, keys_near, values_near)
    keys_half = in_order([keys] + keys_near, "s0")
    values_half = in_order([values] + values_near, "s1")
    keys_far, values_far = ring_start(keys_half, "s1"), ring_start(values_half, "s0")
    keys_far, values_far = meet(sides, keys_far, values_far)
    keys_all = in_order([keys_half] + keys_far, "s1")
    values_all = in_order([values_half] + values_far, "s0").transpose(1, 0, 2, 3)
    return (keys_all.reshape(-1, keys.shape[1]), values_all.reshape(-1, values.shape[1]))


def sequence_scatter(keys, values):
    outer = lax.axis_size("s1")
    width = keys.shape[1]
    keys = keys.reshape(outer, 2, -1, width)
    values = values.reshape(outer, 2, -1, width).transpose(1, 0, 2, 3)
    keys = ring_scatter(ring_scatter(keys, "s1").astype(BF), "s0")
    values = ring_scatter(ring_scatter(values, "s0").astype(BF), "s1")
    return (keys, values)


def routing(expert_ids, slot_rank, capacity):
    rows, top_count = expert_ids.shape
    pairs = expert_ids.reshape(rows * top_count)
    orders = slot_rank.reshape(rows * top_count)
    experts = jnp.arange(EXPERTS, dtype=jnp.int32)
    pair_hot = (pairs[:, None] == experts).astype(BF)
    earlier = (orders[None, :] < orders[:, None]).astype(BF)
    before = jnp.dot(earlier, pair_hot, preferred_element_type=F32)
    hot = pair_hot.astype(F32).reshape(rows, top_count, EXPERTS)
    chosen = jnp.sum(hot, axis=1)
    position = jnp.sum(before.reshape(rows, top_count, EXPERTS) * hot, axis=1)
    held = (chosen > 0.5) & (position < capacity)
    return (jnp.where(held, position, -1.0), chosen > 0.5)


VMEM_BYTES = 44 * 1024 * 1024


def params():
    return pltpu.CompilerParams(vmem_limit_bytes=VMEM_BYTES)


def hint(micros):
    flops = int(micros * 1.15e9 * 0.3)
    return pl.CostEstimate(flops=flops, bytes_accessed=1000, transcendentals=0)


def dot(left, right):
    return jnp.dot(left, right, preferred_element_type=F32)


def dot_lanes(left, right):
    return lax.dot_general(left, right, (((1,), (1,)), ((), ())), preferred_element_type=F32)


def dot_rows(left, right):
    return lax.dot_general(left, right, (((0,), (0,)), ((), ())), preferred_element_type=F32)


REPEATS = HEADS // KV_HEADS


def head_rows(block, which):
    start = which * REPEATS * HEAD_DIM
    return jnp.concatenate(
        [
            block[:, start + k * HEAD_DIM : start + (k + 1) * HEAD_DIM]
            for k in range(REPEATS)
        ],
        axis=0,
    )


def visible(block_start, rows, row_start, prefix_one, shape):
    key_pos = block_start + lax.broadcasted_iota(jnp.int32, shape, 0)
    query_pos = row_start + lax.broadcasted_iota(jnp.int32, shape, 1) % rows
    return (key_pos <= query_pos) | (key_pos < prefix_one)


def attend_kernel(place_ref, q_ref, k_ref, v_ref, o_ref, total_ref):
    rows = q_ref.shape[0]
    prefix_one, row_start = place_ref[0], place_ref[1]
    own_block = row_start // rows
    reach = jnp.maximum(row_start + rows, prefix_one)
    blocks = (reach + rows - 1) // rows
    cols = REPEATS * rows
    outs = []
    totals = []
    q_block = q_ref[...]
    for which in range(2):
        lanes = slice(which * HEAD_DIM, (which + 1) * HEAD_DIM)
        query = head_rows(q_block, which)

        def step(block, carried, masked, lanes=lanes, query=query):
            top, total, acc = carried
            start = pl.multiple_of(block * rows, rows)
            keys = k_ref[pl.ds(start, rows), lanes]
            vals = v_ref[pl.ds(start, rows), lanes]
            score = dot_lanes(keys, query)
            if masked:
                score = jnp.where(
                    visible(start, rows, row_start, prefix_one, score.shape), score, -1e30
                )
            new_top = jnp.maximum(top, jnp.max(score, axis=0, keepdims=True))
            weight = jnp.exp(score - new_top)
            shrink = jnp.exp(top - new_top)
            total = total * shrink + jnp.sum(weight, axis=0, keepdims=True)
            acc = acc * shrink + dot_rows(vals, weight.astype(BF))
            return (new_top, total, acc)

        carried = (
            jnp.full((1, cols), -1e30, F32),
            jnp.zeros((1, cols), F32),
            jnp.zeros((HEAD_DIM, cols), F32),
        )
        carried = lax.fori_loop(0, own_block, functools.partial(step, masked=False), carried)
        carried = lax.fori_loop(own_block, blocks, functools.partial(step, masked=True), carried)
        top, total, acc = carried
        result = (acc / total).T
        log_total = top + jnp.log(total)
        for k in range(REPEATS):
            outs.append(result[k * rows : (k + 1) * rows])
            totals.append(log_total[:, k * rows : (k + 1) * rows])
    o_ref[...] = jnp.concatenate(outs, axis=1).astype(BF)
    total_ref[0] = jnp.concatenate(totals + totals[:2], axis=0)


def attend(query, keys, values, place):
    rows = query.shape[0]
    seq_len = keys.shape[0]
    wide = 2 * REPEATS * HEAD_DIM
    pairs = KV_HEADS // 2
    return pl.pallas_call(
        attend_kernel,
        grid_spec=pltpu.PrefetchScalarGridSpec(
            num_scalar_prefetch=1,
            grid=(pairs,),
            in_specs=[
                pl.BlockSpec((rows, wide), lambda i, p: (0, i)),
                pl.BlockSpec((seq_len, 2 * HEAD_DIM), lambda i, p: (0, i)),
                pl.BlockSpec((seq_len, 2 * HEAD_DIM), lambda i, p: (0, i)),
            ],
            out_specs=[
                pl.BlockSpec((rows, wide), lambda i, p: (0, i)),
                pl.BlockSpec((1, 8, rows), lambda i, p: (i, 0, 0)),
            ],
        ),
        out_shape=[
            jax.ShapeDtypeStruct((rows, Q_WIDTH), BF),
            jax.ShapeDtypeStruct((pairs, 8, rows), F32),
        ],
        compiler_params=params(),
        cost_estimate=hint(36),
        name="attend",
    )(place, query, keys, values)


def attend_back_kernel(
    place_ref, q_ref, k_ref, v_ref, do_ref, o_ref, total_ref, dq_ref, dk_ref, dv_ref
):
    rows = q_ref.shape[0]
    prefix_one, row_start = place_ref[0], place_ref[1]
    own_block = row_start // rows
    reach = jnp.maximum(row_start + rows, prefix_one)
    blocks = (reach + rows - 1) // rows
    cols = REPEATS * rows
    dk_ref[...] = jnp.zeros_like(dk_ref)
    dv_ref[...] = jnp.zeros_like(dv_ref)
    q_block, do_block, o_block = q_ref[...], do_ref[...], o_ref[...]
    grads = []
    for which in range(2):
        lanes = slice(which * HEAD_DIM, (which + 1) * HEAD_DIM)
        query = head_rows(q_block, which)
        grad = head_rows(do_block, which)
        attended = head_rows(o_block, which)
        product = grad.astype(F32) * attended.astype(F32)
        delta = lax.dot_general(
            jnp.ones((8, HEAD_DIM), F32),
            product,
            (((1,), (1,)), ((), ())),
            precision=lax.Precision.HIGHEST,
            preferred_element_type=F32,
        )[:1]
        log_total = jnp.concatenate(
            [total_ref[0, which * REPEATS + k][None, :] for k in range(REPEATS)], axis=1
        )

        def step(
            block,
            acc,
            masked,
            lanes=lanes,
            query=query,
            grad=grad,
            delta=delta,
            log_total=log_total,
        ):
            start = pl.multiple_of(block * rows, rows)
            keys = k_ref[pl.ds(start, rows), lanes]
            vals = v_ref[pl.ds(start, rows), lanes]
            score = dot_lanes(keys, query)
            prob = jnp.exp(score - log_total)
            if masked:
                prob = jnp.where(
                    visible(start, rows, row_start, prefix_one, score.shape), prob, 0.0
                )
            grad_prob = dot_lanes(vals, grad)
            grad_score = (prob * (grad_prob - delta)).astype(BF)
            dv_ref[pl.ds(start, rows), lanes] = dot(prob.astype(BF), grad).astype(BF)
            dk_ref[pl.ds(start, rows), lanes] = dot(grad_score, query).astype(BF)
            return acc + dot_rows(keys, grad_score)

        acc = jnp.zeros((HEAD_DIM, cols), F32)
        acc = lax.fori_loop(0, own_block, functools.partial(step, masked=False), acc)
        acc = lax.fori_loop(own_block, blocks, functools.partial(step, masked=True), acc)
        result = (acc * SCALE).T
        for k in range(REPEATS):
            grads.append(result[k * rows : (k + 1) * rows])
    dq_ref[...] = jnp.concatenate(grads, axis=1).astype(BF)


def attend_back(query, keys, values, grad, attended, log_total, place):
    rows = query.shape[0]
    seq_len = keys.shape[0]
    wide = 2 * REPEATS * HEAD_DIM
    pairs = KV_HEADS // 2
    queries = pl.BlockSpec((rows, wide), lambda i, p: (0, i))
    stripe = pl.BlockSpec((seq_len, 2 * HEAD_DIM), lambda i, p: (0, i))
    return pl.pallas_call(
        attend_back_kernel,
        grid_spec=pltpu.PrefetchScalarGridSpec(
            num_scalar_prefetch=1,
            grid=(pairs,),
            in_specs=[
                queries,
                stripe,
                stripe,
                queries,
                queries,
                pl.BlockSpec((1, 8, rows), lambda i, p: (i, 0, 0)),
            ],
            out_specs=[queries, stripe, stripe],
        ),
        out_shape=[
            jax.ShapeDtypeStruct((rows, Q_WIDTH), BF),
            jax.ShapeDtypeStruct((seq_len, K_WIDTH), BF),
            jax.ShapeDtypeStruct((seq_len, K_WIDTH), BF),
        ],
        compiler_params=params(),
        cost_estimate=hint(54),
        name="attend_back",
    )(place, query, keys, values, grad, attended, log_total)


def slot_rows(positions_row, slots, rows):
    index = lax.broadcasted_iota(jnp.int32, (slots, rows), 0).astype(F32)
    return index == positions_row


def experts_kernel(
    sel_ref,
    own_ref,
    mate_ref,
    gate_ref,
    up_ref,
    down_ref,
    own_part_ref,
    mate_part_ref,
    sent_ref,
    act_ref,
    row_ref,
    inner_ref,
    ret_ref,
):
    rows = own_ref.shape[0]
    width = gate_ref.shape[0]
    local, slots = sent_ref.shape[1:3]
    ff = down_ref.shape[1] // local
    many = 2 * slots
    combines = []
    for p, x_ref in enumerate((own_ref, mate_ref)):
        info = dot_lanes(sel_ref[...], x_ref[:, width:])
        row_ref[p] = info
        parts = []
        for e in range(local):
            hits = slot_rows(info[e : e + 1], slots, rows)
            hot = hits.astype(F32).astype(BF)
            parts.append(jnp.where(hits, info[local + e : local + e + 1], 0.0))
            for n in range(0, width, 512):
                sent_ref[p, e, :, n : n + 512] = dot(hot, x_ref[:, n : n + 512]).astype(BF)
        combines.append(jnp.concatenate(parts, axis=0).T.astype(BF))
    for e in range(local):
        sent = sent_ref[:, e].reshape(many, width)
        for f in range(0, ff, 256):
            lanes = slice(e * ff + f, e * ff + f + 256)
            gate = dot(sent, gate_ref[:, lanes])
            up = dot(sent, up_ref[:, lanes])
            act_ref[:, e, :, f : f + 256] = gate.astype(BF).reshape(2, slots, 256)
            act_ref[:, e, :, ff + f : ff + f + 256] = up.astype(BF).reshape(2, slots, 256)
            inner_ref[:, f : f + 256] = (gate / (1.0 + jnp.exp(-gate)) * up).astype(BF)
        inner = inner_ref[...]
        for n in range(0, width, 512):
            back = dot_lanes(inner, down_ref[n : n + 512, e * ff : (e + 1) * ff])
            ret_ref[:, e * slots : (e + 1) * slots, n : n + 512] = back.astype(BF).reshape(
                2, slots, 512
            )
    for p, part_ref in enumerate((own_part_ref, mate_part_ref)):
        for n in range(0, width, 512):
            part_ref[:, n : n + 512] = dot(combines[p], ret_ref[p, :, n : n + 512]).astype(BF)


def experts(sel, own, mate, weights, slots):
    rows = own.shape[0]
    width, all_ff = weights[2].shape
    local = EXPERTS // 8
    ff = all_ff // local
    return pl.pallas_call(
        experts_kernel,
        out_shape=[
            jax.ShapeDtypeStruct((rows, width), BF),
            jax.ShapeDtypeStruct((rows, width), BF),
            jax.ShapeDtypeStruct((2, local, slots, width), BF),
            jax.ShapeDtypeStruct((2, local, slots, 2 * ff), BF),
            jax.ShapeDtypeStruct((2, 8, rows), F32),
        ],
        scratch_shapes=[
            pltpu.VMEM((2 * slots, ff), BF),
            pltpu.VMEM((2, local * slots, width), BF),
        ],
        compiler_params=params(),
        cost_estimate=hint(12),
        name="experts",
    )(sel, own, mate, *weights)


def experts_back_kernel(
    ids_ref,
    own_ref,
    mate_ref,
    row_ref,
    act_ref,
    gate_ref,
    up_ref,
    down_ref,
    own_back_ref,
    mate_back_ref,
    rows_ref,
    both_ref,
    weighted_ref,
    sent_ref,
):
    rows, width = own_ref.shape
    local, slots = act_ref.shape[1:3]
    ff = down_ref.shape[1] // local
    many = 2 * slots
    hots = []
    for p, grad_ref in enumerate((own_ref, mate_ref)):
        parts = []
        for e in range(local):
            hot = slot_rows(row_ref[p, e : e + 1], slots, rows).astype(F32)
            parts.append(hot)
            for n in range(0, width, 512):
                rows_ref[p, e, :, n : n + 512] = dot(
                    hot.astype(BF), grad_ref[:, n : n + 512]
                ).astype(BF)
        hots.append(parts)
    for e in range(local):
        gates = jnp.concatenate(
            [
                jnp.sum(
                    hots[p][e] * row_ref[p, local + e : local + e + 1], axis=1, keepdims=True
                )
                for p in range(2)
            ],
            axis=0,
        )
        grad = rows_ref[:, e].reshape(many, width)
        slot_grad = jnp.zeros((many, 1), F32)
        for f in range(0, ff, 256):
            through = dot(grad, down_ref[:, e * ff + f : e * ff + f + 256])
            gate = act_ref[:, e, :, f : f + 256].reshape(many, 256).astype(F32)
            up = act_ref[:, e, :, ff + f : ff + f + 256].reshape(many, 256).astype(F32)
            sigmoid = 1.0 / (1.0 + jnp.exp(-gate))
            silu = gate * sigmoid
            inner = silu * up
            slot_grad = slot_grad + jnp.sum(inner * through, axis=1, keepdims=True)
            grad_inner = gates * through
            grad_gate = grad_inner * up * sigmoid * (1.0 + gate * (1.0 - sigmoid))
            both_ref[:, e, :, f : f + 256] = grad_gate.astype(BF).reshape(2, slots, 256)
            both_ref[:, e, :, ff + f : ff + f + 256] = (
                (grad_inner * silu).astype(BF).reshape(2, slots, 256)
            )
            weighted_ref[:, e, :, f : f + 256] = (
                (gates * inner).astype(BF).reshape(2, slots, 256)
            )
        both = both_ref[:, e].reshape(many, 2 * ff)
        lanes = slice(e * ff, (e + 1) * ff)
        for n in range(0, width, 512):
            back = dot_lanes(both[:, :ff], gate_ref[n : n + 512, lanes])
            back = back + dot_lanes(both[:, ff:], up_ref[n : n + 512, lanes])
            sent_ref[:, e * slots : (e + 1) * slots, n : n + 512] = back.astype(BF).reshape(
                2, slots, 512
            )
        high = slot_grad.astype(BF).astype(F32)
        low = slot_grad - high
        lane = lax.broadcasted_iota(jnp.int32, (many, PAD), 1)
        expert = ids_ref[e]
        extra = jnp.where(lane == expert, high, 0.0) + jnp.where(
            lane == expert + EXPERTS, low, 0.0
        )
        sent_ref[:, e * slots : (e + 1) * slots, width:] = extra.astype(BF).reshape(
            2, slots, PAD
        )
    for p, back_ref in enumerate((own_back_ref, mate_back_ref)):
        hot = jnp.concatenate(hots[p], axis=0).T.astype(BF)
        for n in range(0, width, 512):
            back_ref[:, n : n + 512] = dot(hot, sent_ref[p, :, n : n + 512]).astype(BF)
        back_ref[:, width:] = dot(hot, sent_ref[p, :, width:]).astype(BF)


def experts_back(ids, own, mate, kept, weights):
    unused, act, row_info = kept
    rows, width = own.shape
    local, slots = act.shape[1:3]
    ff = weights[2].shape[1] // local
    vmem = pl.BlockSpec(memory_space=pltpu.VMEM)
    return pl.pallas_call(
        experts_back_kernel,
        in_specs=[pl.BlockSpec(memory_space=pltpu.SMEM)] + [vmem] * 7,
        out_shape=[
            jax.ShapeDtypeStruct((rows, width + PAD), BF),
            jax.ShapeDtypeStruct((rows, width + PAD), BF),
            jax.ShapeDtypeStruct((2, local, slots, width), BF),
            jax.ShapeDtypeStruct((2, local, slots, 2 * ff), BF),
            jax.ShapeDtypeStruct((2, local, slots, ff), BF),
        ],
        scratch_shapes=[pltpu.VMEM((2, local * slots, width + PAD), BF)],
        compiler_params=params(),
        cost_estimate=hint(12.5),
        name="experts_back",
    )(ids, own, mate, row_info, act, *weights)


def grads_kernel(*refs):
    count = (len(refs) - 2) // 2
    lefts, rights, out_ref, turned_ref = refs[:count], refs[count:-2], refs[-2], refs[-1]
    members, unused, slots, width = lefts[0].shape
    depth = members * slots

    @pl.when(pl.program_id(1) == 0)
    def turn_once():
        for k, left_ref in enumerate(lefts):
            for n in range(0, width, 256):
                turned_ref[n : n + 256, k * depth : (k + 1) * depth] = (
                    left_ref[:, 0, :, n : n + 256].reshape(depth, 256).T
                )

    right = jnp.concatenate(
        [right_ref[:, 0].reshape(depth, right_ref.shape[3]) for right_ref in rights], axis=0
    )

    def rows_of(index, unused):
        start = pl.multiple_of(index * 256, 256)
        out_ref[0, pl.ds(start, 256), :] = dot(turned_ref[pl.ds(start, 256), :], right).astype(BF)
        return unused

    lax.fori_loop(0, width // 256, rows_of, 0)


def expert_grads(lefts, rights):
    members, local, slots, width = lefts[0].shape
    cols = rights[0].shape[3]
    step = FF
    count = len(lefts)
    return pl.pallas_call(
        grads_kernel,
        grid=(local, cols // step),
        in_specs=[pl.BlockSpec((members, 1, slots, width), lambda e, n: (0, e, 0, 0))] * count
        + [pl.BlockSpec((members, 1, slots, step), lambda e, n: (0, e, 0, n))] * count,
        out_specs=pl.BlockSpec((1, width, step), lambda e, n: (n, 0, e)),
        out_shape=jax.ShapeDtypeStruct((cols // step, width, local * step), BF),
        scratch_shapes=[pltpu.VMEM((width, count * members * slots), BF)],
        compiler_params=params(),
        cost_estimate=hint(9 * local * cols // FF),
        name="expert_grads",
    )(*lefts, *rights)


def attention_in(hidden_in, lead, rotation, sides):
    query_full, key_value_full, unused, gain_one, unused = lead
    hat_one, factor_one = normalize(hidden_in)
    normed_one = (hat_one * gain_one[None, :]).astype(BF)
    mixed = dot(normed_one, key_value_full)
    keys_here = rotate(mixed[:, :K_WIDTH], rotation, 1.0).astype(BF)
    keys_all, values_all = sequence_gather(keys_here, mixed[:, K_WIDTH:].astype(BF), sides)
    query = dot(normed_one, query_full)
    query = rotate(query, rotation, 1.0).astype(BF) * jnp.asarray(SCALE, BF)
    return ((query, keys_all, values_all), (hat_one, factor_one, normed_one))


def attention_out(hidden_in, attended, out_full, lead, routes):
    router_full, gain_two = lead[2], lead[4]
    positions, chosen_mask, sel, ids, slots = routes
    rows = hidden_in.shape[0]
    hidden = hidden_in + dot_lanes(attended, out_full)
    hat_two, factor_two = normalize(hidden)
    normed_two = (hat_two * gain_two[None, :]).astype(BF)
    logits = dot(normed_two, router_full)
    gates = jax.nn.softmax(jnp.where(chosen_mask, logits, -jnp.inf), axis=-1)
    extra = jnp.concatenate(
        [gates.astype(BF), positions.astype(BF), jnp.zeros((rows, PAD - 2 * EXPERTS), BF)], axis=1
    )
    message = jnp.concatenate([normed_two, extra], axis=1)
    return (hidden, message, (hat_two, factor_two, normed_two, gates))


def norm_two_grad(grad_result, back, kept, lead):
    hat_two, factor_two, normed_two, gates = kept
    router_full, gain_two = lead[2], lead[4]
    width = grad_result.shape[1]
    gate_grad = back[:, width : width + EXPERTS] + back[:, width + EXPERTS : width + 2 * EXPERTS]
    grad_logits = (gates * (gate_grad - jnp.sum(gates * gate_grad, axis=-1, keepdims=True))).astype(
        BF
    )
    router_term = dot_rows(grad_logits, normed_two)
    grad_normed_two = back[:, :width] + dot_lanes(grad_logits, router_full)
    gain_two_term = jnp.sum(hat_two * grad_normed_two, axis=0)
    grad_hat_two = grad_normed_two * gain_two[None, :]
    grad_hidden = grad_result + norm_back(grad_hat_two, hat_two, factor_two)
    return (grad_hidden, router_term, gain_two_term)


def to_rows(term):
    return lax.psum_scatter(term.astype(BF), ALL_AXES, scatter_dimension=0, tiled=True)


def norm_one_grad(grad_hidden, grad_mixed, kept, lead):
    hat_one, factor_one, normed_one = kept
    query_full, key_value_full, unused, gain_one, unused = lead
    grad_normed_one = dot_lanes(grad_mixed[:, :Q_WIDTH], query_full)
    grad_normed_one = grad_normed_one + dot_lanes(grad_mixed[:, Q_WIDTH:], key_value_full)
    gain_one_term = jnp.sum(hat_one * grad_normed_one, axis=0)
    grad_hat_one = grad_normed_one * gain_one[None, :]
    return (grad_hidden + norm_back(grad_hat_one, hat_one, factor_one), gain_one_term)


FETCH0 = ("h0", "x0", "y0 h1", "x1 h2", "y1 x2")
FETCH1 = ("", "h0", "h1 x0", "", "h2 y0", "x1", "y1 x2")
DOWN1 = ("", "y0", "x0", "h0")
IN1 = ("y0", "y1 x0", "x1 h0", "", "h1")
DOWN0 = ("", "y0", "x0")
IN0 = ("", "y0", "y1 x0")


def local(
    tokens,
    cotangent,
    prefix_len,
    expert_ids,
    slot_rank,
    norm1_gain,
    qkv_weight,
    out_weight,
    norm2_gain,
    router_weight,
    in_weight,
    down_weight,
):
    groups, rows, width = tokens.shape
    row_start = lax.axis_index(SEQ_AXES) * rows
    capacity = (5 * rows * TOP + 4 * EXPERTS - 1) // (4 * EXPERTS)
    slots = (capacity + 15) // 16 * 16
    positions, chosen_mask = routing(expert_ids[0], slot_rank[0, 0], capacity)
    fsdp = lax.axis_size(FSDP_AXES)
    stored = EXPERTS // fsdp
    high = lax.axis_size("fh")
    mine = []
    for high_index in range(high // 2):
        for within in range(stored):
            owner = (lax.axis_index("s0") * (high // 2) + high_index) * 4
            owner = owner + lax.axis_index("fl") * 2 + lax.axis_index("c")
            mine.append(owner * stored + within)
    ids = jnp.stack(mine).astype(jnp.int32)
    lanes = jnp.arange(PAD)[None, :]
    sel = jnp.concatenate(
        [
            (lanes == ids[:, None] + EXPERTS).astype(BF),
            (lanes == ids[:, None]).astype(BF),
            jnp.zeros((8 - 2 * len(mine), PAD), BF),
        ],
        axis=0,
    )
    routes = (positions, chosen_mask, sel, ids, slots)
    rotation = tables(row_start + jnp.arange(rows, dtype=jnp.int32))
    place = jnp.stack([prefix_len[0], row_start]).astype(jnp.int32)
    part_rows = qkv_weight.shape[1]
    weight_rows = in_weight.shape[1]

    def lead_part(index):
        return jnp.concatenate(
            [
                qkv_weight[index],
                router_weight[index],
                norm1_gain[index][:, None],
                norm2_gain[index][:, None],
                jnp.zeros((part_rows, PAD - EXPERTS - 2), BF),
            ],
            axis=1,
        )

    def gather_all(part):
        return lax.all_gather(part, ALL_AXES, axis=0, tiled=True)

    def split_lead(lead):
        wide = Q_WIDTH + 2 * K_WIDTH
        return (
            lead[:, :Q_WIDTH],
            lead[:, Q_WIDTH:wide],
            lead[:, wide : wide + EXPERTS],
            lead[:, wide + EXPERTS].astype(F32),
            lead[:, wide + EXPERTS + 1].astype(F32),
        )

    def expert_parts(index):
        part = in_weight[index]
        gates = [part[:, e * 2 * FF : e * 2 * FF + FF] for e in range(stored)]
        ups = [part[:, e * 2 * FF + FF : (e + 1) * 2 * FF] for e in range(stored)]
        return [
            jnp.concatenate(gates, axis=1),
            jnp.concatenate(ups, axis=1),
            down_weight[index],
        ]

    def forward_experts(weights):
        return lambda own, mate: experts(sel, own, mate, weights, slots)

    def backward_experts(weights, kept):
        chips = iter(kept)
        return lambda own, mate: experts_back(ids, own, mate, next(chips), weights)

    def down_grads(kept):
        return expert_grads([chip[0] for chip in kept], [chip[2] for chip in kept])[0]

    def in_grads(sents, kept):
        both = expert_grads([chip[0] for chip in sents], [chip[1] for chip in kept])
        return [both[0], both[1]]

    def follow(hops, count, plan):
        names = [name for name in hops if name != "from"]
        state = {k: hops["from"][k] for k in range(count)}
        begun = {}

        def begin(name, k):
            if (name, k) not in begun:
                begun[name, k] = hops[name][0](state[k])

        def finish(name, k, raw):
            state[k] = hops[name][1](state[k], raw)

        done = set()
        for stretch in plan:
            ends = []
            for word in stretch.split():
                name, k = word[-2], int(word[-1])
                begin(name, k)
                if word[0] != "+":
                    ends.append((name, k))
            raws = yield [begun[end] for end in ends]
            for (name, k), raw in zip(ends, raws):
                finish(name, k, raw)
                done.add((name, k))
        for name in names:
            for k in range(count):
                if (name, k) not in done:
                    begin(name, k)
                    finish(name, k, begun[name, k])
        return [state[k] for k in range(count)]

    def fetch(parts, plan):
        hops = {
            "from": parts,
            "h": (lambda part: ring_start(part, "fh"), high_end),
            "x": (lambda pair: swap(pair[1], "s0"), lambda pair, raw: low_end(pair[0], raw)),
            "y": (lambda block: ring_start(block, "s1"), rows_end),
        }
        return follow(hops, len(parts), plan)

    def deliver(terms, plan):
        hops = {
            "from": [by_rows(term) for term in terms],
            "y": (
                lambda blocks: scatter_start(blocks, "s1"),
                lambda blocks, raw: low_split(scatter_end(blocks, raw, "s1").astype(BF)),
            ),
            "x": (lambda pair: swap(pair[1], "s0"), lambda pair, raw: all_high(pair[0], raw)),
            "h": (
                lambda blocks: scatter_start(blocks, "fh"),
                lambda blocks, raw: scatter_end(blocks, raw, "fh"),
            ),
        }
        return follow(hops, len(terms), plan)

    stream = tokens.astype(F32).reshape(rows, width)
    lead0 = gather_all(lead_part(0))
    lead0, parts, out_part = tie(lead0, expert_parts(0), out_weight[0])
    fetch0 = Side(fetch(parts, FETCH0))
    out0 = lax.all_gather(out_part, FSDP_AXES, axis=0, tiled=True)
    out0 = lax.all_gather(out0, SEQ_AXES, axis=0, tiled=True)
    lead0 = split_lead(lead0)
    ready0, kept_one0 = attention_in(stream, lead0, rotation, [fetch0])
    ready0 = meet([fetch0], ready0)
    attended0, total0 = attend(*ready0, place)
    attended0 = meet([fetch0], attended0)
    hidden0, message0, kept_two0 = attention_out(stream, attended0, out0, lead0, routes)
    message0, lead_next, out_next, parts = meet(
        [fetch0], message0, lead_part(1), out_weight[1], expert_parts(1)
    )
    fetch1 = Side(fetch(parts, FETCH1))
    lead1, out1 = gather_all(lead_next), gather_all(out_next)
    weights0 = fetch0.result
    merged, kept_experts0, unused, unused = through_experts(
        message0, forward_experts(weights0), [fetch1]
    )
    stream1 = hidden0 + merged
    lead1 = split_lead(lead1)
    ready1, kept_one1 = attention_in(stream1, lead1, rotation, [fetch1])
    ready1, grad = meet([fetch1], ready1, cotangent)
    attended1, total1 = attend(*ready1, place)
    attended1 = meet([fetch1], attended1)
    hidden1, message1, kept_two1 = attention_out(stream1, attended1, out1, lead1, routes)
    message1 = meet([fetch1], message1)
    while fetch1.result is None:
        meet([fetch1])
    weights1 = fetch1.result
    forward1 = forward_experts(weights1)
    own, near, low, far, unused, unused = on_chip_pairs(message1, forward1, [])
    far = forward1(far, swap(far, "c"))
    chips1 = [own, near, low, far]
    kept_experts1 = [chip[2:] for chip in chips1]

    def attention_grad(grad_hidden, ready, attended, total, out_full, sides):
        grad_branch = grad_hidden.astype(BF)
        grad_attended = dot(grad_branch, out_full).astype(BF)
        out_term = dot_rows(grad_branch, attended).astype(BF)
        grad_attended, out_term = meet(sides, grad_attended, out_term)
        grads = attend_back(*ready, grad_attended, attended, total, place)
        share = to_rows(out_term)
        return (share, meet(sides, grads))

    def mixed_grad(grads, sides, extra):
        grad_query, grad_keys, grad_values = grads
        sums = sequence_scatter(grad_keys, grad_values)
        (key_sums, value_sums), extra = meet(sides, sums, extra)
        grad_query = rotate(grad_query.astype(F32), rotation, -1.0)
        grad_keys = rotate(rounded(key_sums), rotation, -1.0)
        return (
            jnp.concatenate([grad_query, grad_keys, value_sums], axis=-1).astype(BF),
            extra,
        )

    back1, kept, down_term, unused = through_experts(
        grad.reshape(rows, width),
        backward_experts(weights1, kept_experts1),
        [],
        late=down_grads,
    )
    back1, pairs1 = tie(back1, [chip[:2] for chip in chips1])
    output = hidden1 + chip_sums_home(*pairs1)
    grad = grad.astype(F32).reshape(rows, width)
    down_side1 = Side(deliver([down_term], DOWN1))
    grad_hidden1, router1, gain_two1 = norm_two_grad(grad, back1, kept_two1, lead1)
    out_share1, grads = attention_grad(
        grad_hidden1, ready1, attended1, total1, out1, [down_side1]
    )
    grads, kept, output = tie(grads, kept, output)
    output = output.reshape(groups, rows, width).astype(BF)
    grad_mixed1, (in_terms, out_share1) = mixed_grad(
        grads, [down_side1], (in_grads(kept_experts1, kept), out_share1)
    )
    in_side1 = Side(deliver(in_terms, IN1))
    qkv_term = dot_rows(kept_one1[2], grad_mixed1).astype(BF)
    grad, gain_one1 = norm_one_grad(grad_hidden1, grad_mixed1, kept_one1, lead1)
    grad, qkv_term = tie(grad, qkv_term)
    qkv_share1 = to_rows(qkv_term)

    side1 = [down_side1, in_side1]
    back0, unused, (down_term, qkv_share1), in_terms = through_experts(
        grad.astype(BF),
        backward_experts(weights0, kept_experts0),
        side1,
        late=lambda kept: (down_grads(kept), qkv_share1),
        last=lambda kept: in_grads(kept_experts0, kept),
    )
    down_side0 = Side(deliver([down_term], DOWN0))
    in_side0 = Side(deliver(in_terms, IN0))
    sides = side1 + [down_side0, in_side0]
    grad_hidden0, router0, gain_two0 = norm_two_grad(grad, back0, kept_two0, lead0)
    out_share0, grads = attention_grad(
        grad_hidden0, ready0, attended0, total0, out0, sides
    )
    grad_mixed0, out_share0 = mixed_grad(grads, sides, out_share0)
    grad, gain_one0 = norm_one_grad(grad_hidden0, grad_mixed0, kept_one0, lead0)
    while any(side.result is None for side in sides):
        meet(sides)
    gate_share1, up_share1 = in_side1.result
    gate_share0, up_share0 = in_side0.result
    down_share1, down_share0 = down_side1.result[0], down_side0.result[0]
    gains = jnp.stack([gain_one0, gain_one1, gain_two0, gain_two1])
    smalls = jnp.concatenate(
        [router0, router1, jnp.pad(gains, ((0, PAD - 2 * EXPERTS - 4), (0, 0)))], axis=0
    ).astype(BF)
    left = jnp.concatenate([kept_one0[2], smalls], axis=0)
    right = jnp.concatenate(
        [
            jnp.pad(grad_mixed0, ((0, 0), (0, PAD))),
            jnp.pad(jnp.eye(PAD, dtype=BF), ((0, 0), (Q_WIDTH + 2 * K_WIDTH, 0))),
        ],
        axis=0,
    )
    rest = to_rows(dot_rows(left, right))
    smalls = rest[:, Q_WIDTH + 2 * K_WIDTH :].astype(F32)
    routers = jnp.stack([smalls[:, :EXPERTS], smalls[:, EXPERTS : 2 * EXPERTS]])
    gains = smalls[:, 2 * EXPERTS : 2 * EXPERTS + 4].T
    qkv_share0 = rest[:, : Q_WIDTH + 2 * K_WIDTH]

    def in_share(gate, up):
        columns = []
        for e in range(stored):
            columns += [gate[:, e * FF : (e + 1) * FF], up[:, e * FF : (e + 1) * FF]]
        return jnp.concatenate(columns, axis=1)

    return (
        output,
        grad.reshape(groups, rows, width),
        gains[:2],
        jnp.stack([qkv_share0, qkv_share1]).astype(F32),
        jnp.stack([out_share0, out_share1]).astype(F32),
        gains[2:],
        routers,
        jnp.stack([in_share(gate_share0, up_share0), in_share(gate_share1, up_share1)]),
        jnp.stack([down_share0, down_share1]),
    )


def solution(mesh):
    seq, fsdp = mesh.devices.shape
    inner_mesh = Mesh(mesh.devices.reshape(seq // 2, 2, fsdp // 4, 2, 2), ALL_AXES)
    rows = P(None, ALL_AXES)
    flat = P(None, ALL_AXES, None)
    expert = P(None, SEQ_AXES, FSDP_AXES)
    token = P(FSDP_AXES, SEQ_AXES, None)
    return jax.shard_map(
        local,
        mesh=inner_mesh,
        in_specs=(
            token,
            token,
            P(FSDP_AXES),
            token,
            token,
            rows,
            flat,
            flat,
            rows,
            flat,
            expert,
            expert,
        ),
        out_specs=(token, token, rows, flat, flat, rows, flat, expert, expert),
        check_vma=False,
    )
```

```python
import functools

import jax
import jax.numpy as jnp
from jax import lax
from jax.experimental import pallas as pl
from jax.experimental.pallas import tpu as pltpu
from jax.sharding import Mesh
from jax.sharding import PartitionSpec as P

HEADS = 24
KV_HEADS = 8
HEAD_DIM = 64
FF = 512
TOP = 8
EXPERTS = 16
LAYERS = 2
EPS = 1e-06
THETA = 10000.0
SCALE = 0.125
Q_WIDTH = HEADS * HEAD_DIM
K_WIDTH = KV_HEADS * HEAD_DIM
PAD = 128
SEQ_AXES = ("s1", "s0")
FSDP_AXES = ("fh", "fl", "c")
ALL_AXES = SEQ_AXES + FSDP_AXES
BF = jnp.bfloat16
F32 = jnp.float32


def normalize(values):
    factor = lax.rsqrt(jnp.mean(values * values, axis=-1, keepdims=True) + EPS)
    return (values * factor, factor)


def norm_back(grad_hat, hat_values, factor):
    inner = jnp.mean(grad_hat * hat_values, axis=-1, keepdims=True)
    return factor * (grad_hat - hat_values * inner)


def tables(positions):
    steps = jnp.arange(HEAD_DIM // 2, dtype=F32)
    freqs = THETA ** (-2.0 * steps / HEAD_DIM)
    angles = positions.astype(F32)[:, None] * freqs[None, :]
    cosine, sine = jnp.cos(angles), jnp.sin(angles)
    none = jnp.zeros_like(sine)
    return (
        jnp.concatenate([cosine, cosine], axis=-1),
        jnp.concatenate([-sine, none], axis=-1),
        jnp.concatenate([none, sine], axis=-1),
    )


def rotate(values, rotation, sign):
    cosine, ahead, behind = (
        jnp.tile(table, (1, values.shape[1] // HEAD_DIM)) for table in rotation
    )
    half = HEAD_DIM // 2
    later = jnp.roll(values, -half, axis=1)
    sooner = jnp.roll(values, half, axis=1)
    return values * cosine + sign * (later * ahead + sooner * behind)


def rounded(values):
    return lax.optimization_barrier(values.astype(BF)).astype(F32)


def swap(values, axis):
    return lax.ppermute(values, axis, [(0, 1), (1, 0)])


def tie(*values):
    return lax.optimization_barrier(values)


class Side:
    def __init__(self, steps):
        self.steps = steps
        self.result = None
        self.advance(None)

    def advance(self, value):
        if self.result is not None:
            return
        try:
            self.pending = self.steps.send(value)
        except StopIteration as stop:
            self.pending, self.result = (), stop.value


def meet(sides, *values):
    pending, values = tie([side.pending for side in sides], values)
    for side, value in zip(sides, pending):
        side.advance(value)
    return values[0] if len(values) == 1 else values


def ring_start(values, axis):
    size = lax.axis_size(axis)
    blocks = []
    for step in range(1, size):
        values = lax.ppermute(values, axis, [(i, (i + 1) % size) for i in range(size)])
        blocks.append(values)
    return blocks


def in_order(blocks, axis):
    size = len(blocks)
    index = lax.axis_index(axis)
    if size == 2:
        first = index == 0
        return jnp.stack(
            [jnp.where(first, blocks[0], blocks[1]), jnp.where(first, blocks[1], blocks[0])]
        )
    result = jnp.zeros((size,) + blocks[0].shape, blocks[0].dtype)
    for step, block in enumerate(blocks):
        result = lax.dynamic_update_index_in_dim(result, block, (index - step) % size, 0)
    return result


def ring_gather(values, axis):
    return in_order([values] + ring_start(values, axis), axis)


def pick(blocks, index):
    return lax.dynamic_index_in_dim(blocks, index, 0, False)


def scatter_start(blocks, axis):
    size = lax.axis_size(axis)
    index = lax.axis_index(axis)
    carried = pick(blocks, (index + size - 1) % size)
    for step in range(1, size):
        carried = lax.ppermute(carried, axis, [(i, (i + 1) % size) for i in range(size)])
        if step < size - 1:
            mine = pick(blocks, (index + size - 1 - step) % size)
            carried = (carried.astype(F32) + mine.astype(F32)).astype(BF)
    return carried


def scatter_end(blocks, carried, axis):
    return carried.astype(F32) + pick(blocks, lax.axis_index(axis)).astype(F32)


def ring_scatter(blocks, axis):
    return scatter_end(blocks, scatter_start(blocks, axis), axis)


def high_end(part, received):
    rows, cols = part.shape
    high = lax.axis_size("fh")
    low_index = lax.axis_index("s0")
    if high == 2:
        same = lax.axis_index("fh") == low_index
        return (jnp.where(same, part, received[0]), jnp.where(same, received[0], part))
    blocks = in_order([part] + received, "fh").reshape(2, high // 2, rows, cols)
    join = lambda these: these.transpose(1, 0, 2).reshape(rows, high // 2 * cols)
    return (join(pick(blocks, low_index)), join(pick(blocks, 1 - low_index)))


def low_end(keep, received):
    rows, cols = keep.shape
    return in_order([keep, received], "s0").reshape(2 * rows, cols)


def rows_end(block, received):
    return in_order([block] + received, "s1").reshape(-1, block.shape[1])


def by_rows(full):
    return full.reshape(lax.axis_size("s1"), -1, full.shape[1])


def low_split(summed):
    high = lax.axis_size("fh")
    rows = summed.shape[0] // 2
    cols = summed.shape[1] // (high // 2)
    low_index = lax.axis_index("s0")
    halves = summed.reshape(2, rows, high // 2, cols).transpose(0, 2, 1, 3)
    return (pick(halves, low_index), pick(halves, 1 - low_index))


def all_high(keep, received):
    both = in_order([keep, received], "s0")
    return both.reshape((lax.axis_size("fh"),) + keep.shape[1:])


def on_chip_pairs(message, on_chip, sides):
    half = message.shape[0] // 2
    near = swap(message, "s0")
    low = swap(message, "fl")
    own = on_chip(message, swap(message, "c"))
    near, low, own = meet(sides, near, low, own)
    far_top = swap(low[:half], "s0")
    far_bottom = swap(near[half:], "fl")
    near_mate, low_mate = tie(swap(near, "c"), swap(low, "c"))
    near, low = tie(on_chip(near, near_mate), low)
    near_sum = swap(near[1], "c")
    own_sum = swap(own[1], "c")
    low = on_chip(low, low_mate)
    far_top, far_bottom, low, near_sum, own_sum = meet(
        sides, far_top, far_bottom, low, near_sum, own_sum
    )
    far = jnp.concatenate([far_top, far_bottom], axis=0)
    return (own, near, low, far, own_sum, near_sum)


def sums_home(own, near, low, far, own_sum, near_sum, on_chip, sides, late=None, last=None):
    half = far.shape[0] // 2
    far_mate = swap(far, "c")
    low_sum = swap(low[1], "c")
    near_sum = near[0].astype(F32) + near_sum.astype(F32)
    near_top = swap(near_sum[:half].astype(BF), "s0")
    far_mate, low_sum = tie(far_mate, low_sum)
    low_sum = low[0].astype(F32) + low_sum.astype(F32)
    low_bottom = swap(low_sum[half:].astype(BF), "fl")
    far = on_chip(far, far_mate)
    near_top, low_bottom, far = tie(near_top, low_bottom, far)
    far_sum = (far[0].astype(F32) + swap(far[1], "c").astype(F32)).astype(BF)
    kept = [own[2:], near[2:], low[2:], far[2:]]
    far_top = swap(far_sum[:half], "s0")
    far_bottom = swap(far_sum[half:], "fl")
    if late is not None:
        late = late(kept)
    far_top, far_bottom, late = tie(far_top, far_bottom, late)
    near_bottom = swap((near_sum[half:] + far_bottom.astype(F32)).astype(BF), "s0")
    low_top = swap((low_sum[:half] + far_top.astype(F32)).astype(BF), "fl")
    if last is not None:
        last = last(kept)
    near_bottom, low_top, last = meet(sides, near_bottom, low_top, last)
    own_sum = own[0].astype(F32) + own_sum.astype(F32)
    top = own_sum[:half] + near_top.astype(F32) + low_top.astype(F32)
    bottom = own_sum[half:] + near_bottom.astype(F32) + low_bottom.astype(F32)
    return (jnp.concatenate([top, bottom], axis=0), kept, late, last)


def through_experts(message, on_chip, sides, late=None, last=None):
    return sums_home(
        *on_chip_pairs(message, on_chip, sides), on_chip, sides, late=late, last=last
    )


def chip_sums_home(own, near, low, far):
    half = own[0].shape[0] // 2
    own, near, low, far = (
        pair[0].astype(F32) + swap(pair[1], "c").astype(F32) for pair in (own, near, low, far)
    )
    far = far.astype(BF)
    far_top = swap(far[:half], "s0").astype(F32)
    far_bottom = swap(far[half:], "fl").astype(F32)
    near = jnp.concatenate([near[:half], near[half:] + far_bottom], axis=0).astype(BF)
    low = jnp.concatenate([low[:half] + far_top, low[half:]], axis=0).astype(BF)
    return own + swap(near, "s0").astype(F32) + swap(low, "fl").astype(F32)


def sequence_gather(keys, values, sides):
    keys_near, values_near = ring_start(keys, "s0"), ring_start(values, "s1")
    keys_near, values_near = meet(sides, keys_near, values_near)
    keys_half = in_order([keys] + keys_near, "s0")
    values_half = in_order([values] + values_near, "s1")
    keys_far, values_far = ring_start(keys_half, "s1"), ring_start(values_half, "s0")
    keys_far, values_far = meet(sides, keys_far, values_far)
    keys_all = in_order([keys_half] + keys_far, "s1")
    values_all = in_order([values_half] + values_far, "s0").transpose(1, 0, 2, 3)
    return (keys_all.reshape(-1, keys.shape[1]), values_all.reshape(-1, values.shape[1]))


def sequence_scatter(keys, values):
    outer = lax.axis_size("s1")
    width = keys.shape[1]
    keys = keys.reshape(outer, 2, -1, width)
    values = values.reshape(outer, 2, -1, width).transpose(1, 0, 2, 3)
    keys = ring_scatter(ring_scatter(keys, "s1").astype(BF), "s0")
    values = ring_scatter(ring_scatter(values, "s0").astype(BF), "s1")
    return (keys, values)


def routing(expert_ids, slot_rank, capacity):
    rows, top_count = expert_ids.shape
    pairs = expert_ids.reshape(rows * top_count)
    orders = slot_rank.reshape(rows * top_count)
    experts = jnp.arange(EXPERTS, dtype=jnp.int32)
    pair_hot = (pairs[:, None] == experts).astype(BF)
    earlier = (orders[None, :] < orders[:, None]).astype(BF)
    before = jnp.dot(earlier, pair_hot, preferred_element_type=F32)
    hot = pair_hot.astype(F32).reshape(rows, top_count, EXPERTS)
    chosen = jnp.sum(hot, axis=1)
    position = jnp.sum(before.reshape(rows, top_count, EXPERTS) * hot, axis=1)
    held = (chosen > 0.5) & (position < capacity)
    return (jnp.where(held, position, -1.0), chosen > 0.5)


VMEM_BYTES = 44 * 1024 * 1024


def params():
    return pltpu.CompilerParams(vmem_limit_bytes=VMEM_BYTES)


def hint(micros):
    flops = int(micros * 1.15e9 * 0.3)
    return pl.CostEstimate(flops=flops, bytes_accessed=1000, transcendentals=0)


def dot(left, right):
    return jnp.dot(left, right, preferred_element_type=F32)


def dot_lanes(left, right):
    return lax.dot_general(left, right, (((1,), (1,)), ((), ())), preferred_element_type=F32)


def dot_rows(left, right):
    return lax.dot_general(left, right, (((0,), (0,)), ((), ())), preferred_element_type=F32)


REPEATS = HEADS // KV_HEADS


def head_rows(block, which):
    start = which * REPEATS * HEAD_DIM
    return jnp.concatenate(
        [
            block[:, start + k * HEAD_DIM : start + (k + 1) * HEAD_DIM]
            for k in range(REPEATS)
        ],
        axis=0,
    )


def visible(block_start, rows, row_start, prefix_one, shape):
    key_pos = block_start + lax.broadcasted_iota(jnp.int32, shape, 0)
    query_pos = row_start + lax.broadcasted_iota(jnp.int32, shape, 1) % rows
    return (key_pos <= query_pos) | (key_pos < prefix_one)


def attend_kernel(place_ref, q_ref, k_ref, v_ref, o_ref, total_ref):
    rows = q_ref.shape[0]
    prefix_one, row_start = place_ref[0], place_ref[1]
    own_block = row_start // rows
    reach = jnp.maximum(row_start + rows, prefix_one)
    blocks = (reach + rows - 1) // rows
    cols = REPEATS * rows
    outs = []
    totals = []
    q_block = q_ref[...]
    for which in range(2):
        lanes = slice(which * HEAD_DIM, (which + 1) * HEAD_DIM)
        query = head_rows(q_block, which)

        def step(block, carried, masked, lanes=lanes, query=query):
            top, total, acc = carried
            start = pl.multiple_of(block * rows, rows)
            keys = k_ref[pl.ds(start, rows), lanes]
            vals = v_ref[pl.ds(start, rows), lanes]
            score = dot_lanes(keys, query)
            if masked:
                score = jnp.where(
                    visible(start, rows, row_start, prefix_one, score.shape), score, -1e30
                )
            new_top = jnp.maximum(top, jnp.max(score, axis=0, keepdims=True))
            weight = jnp.exp(score - new_top)
            shrink = jnp.exp(top - new_top)
            total = total * shrink + jnp.sum(weight, axis=0, keepdims=True)
            acc = acc * shrink + dot_rows(vals, weight.astype(BF))
            return (new_top, total, acc)

        carried = (
            jnp.full((1, cols), -1e30, F32),
            jnp.zeros((1, cols), F32),
            jnp.zeros((HEAD_DIM, cols), F32),
        )
        carried = lax.fori_loop(0, own_block, functools.partial(step, masked=False), carried)
        carried = lax.fori_loop(own_block, blocks, functools.partial(step, masked=True), carried)
        top, total, acc = carried
        result = (acc / total).T
        log_total = top + jnp.log(total)
        for k in range(REPEATS):
            outs.append(result[k * rows : (k + 1) * rows])
            totals.append(log_total[:, k * rows : (k + 1) * rows])
    o_ref[...] = jnp.concatenate(outs, axis=1).astype(BF)
    total_ref[0] = jnp.concatenate(totals + totals[:2], axis=0)


def attend(query, keys, values, place):
    rows = query.shape[0]
    seq_len = keys.shape[0]
    wide = 2 * REPEATS * HEAD_DIM
    pairs = KV_HEADS // 2
    return pl.pallas_call(
        attend_kernel,
        grid_spec=pltpu.PrefetchScalarGridSpec(
            num_scalar_prefetch=1,
            grid=(pairs,),
            in_specs=[
                pl.BlockSpec((rows, wide), lambda i, p: (0, i)),
                pl.BlockSpec((seq_len, 2 * HEAD_DIM), lambda i, p: (0, i)),
                pl.BlockSpec((seq_len, 2 * HEAD_DIM), lambda i, p: (0, i)),
            ],
            out_specs=[
                pl.BlockSpec((rows, wide), lambda i, p: (0, i)),
                pl.BlockSpec((1, 8, rows), lambda i, p: (i, 0, 0)),
            ],
        ),
        out_shape=[
            jax.ShapeDtypeStruct((rows, Q_WIDTH), BF),
            jax.ShapeDtypeStruct((pairs, 8, rows), F32),
        ],
        compiler_params=params(),
        cost_estimate=hint(36),
        name="attend",
    )(place, query, keys, values)


def attend_back_kernel(
    place_ref, q_ref, k_ref, v_ref, do_ref, o_ref, total_ref, dq_ref, dk_ref, dv_ref
):
    rows = q_ref.shape[0]
    prefix_one, row_start = place_ref[0], place_ref[1]
    own_block = row_start // rows
    reach = jnp.maximum(row_start + rows, prefix_one)
    blocks = (reach + rows - 1) // rows
    cols = REPEATS * rows
    dk_ref[...] = jnp.zeros_like(dk_ref)
    dv_ref[...] = jnp.zeros_like(dv_ref)
    q_block, do_block, o_block = q_ref[...], do_ref[...], o_ref[...]
    grads = []
    for which in range(2):
        lanes = slice(which * HEAD_DIM, (which + 1) * HEAD_DIM)
        query = head_rows(q_block, which)
        grad = head_rows(do_block, which)
        attended = head_rows(o_block, which)
        product = grad.astype(F32) * attended.astype(F32)
        delta = lax.dot_general(
            jnp.ones((8, HEAD_DIM), F32),
            product,
            (((1,), (1,)), ((), ())),
            precision=lax.Precision.HIGHEST,
            preferred_element_type=F32,
        )[:1]
        log_total = jnp.concatenate(
            [total_ref[0, which * REPEATS + k][None, :] for k in range(REPEATS)], axis=1
        )

        def step(
            block,
            acc,
            masked,
            lanes=lanes,
            query=query,
            grad=grad,
            delta=delta,
            log_total=log_total,
        ):
            start = pl.multiple_of(block * rows, rows)
            keys = k_ref[pl.ds(start, rows), lanes]
            vals = v_ref[pl.ds(start, rows), lanes]
            score = dot_lanes(keys, query)
            prob = jnp.exp(score - log_total)
            if masked:
                prob = jnp.where(
                    visible(start, rows, row_start, prefix_one, score.shape), prob, 0.0
                )
            grad_prob = dot_lanes(vals, grad)
            grad_score = (prob * (grad_prob - delta)).astype(BF)
            dv_ref[pl.ds(start, rows), lanes] = dot(prob.astype(BF), grad).astype(BF)
            dk_ref[pl.ds(start, rows), lanes] = dot(grad_score, query).astype(BF)
            return acc + dot_rows(keys, grad_score)

        acc = jnp.zeros((HEAD_DIM, cols), F32)
        acc = lax.fori_loop(0, own_block, functools.partial(step, masked=False), acc)
        acc = lax.fori_loop(own_block, blocks, functools.partial(step, masked=True), acc)
        result = (acc * SCALE).T
        for k in range(REPEATS):
            grads.append(result[k * rows : (k + 1) * rows])
    dq_ref[...] = jnp.concatenate(grads, axis=1).astype(BF)


def attend_back(query, keys, values, grad, attended, log_total, place):
    rows = query.shape[0]
    seq_len = keys.shape[0]
    wide = 2 * REPEATS * HEAD_DIM
    pairs = KV_HEADS // 2
    queries = pl.BlockSpec((rows, wide), lambda i, p: (0, i))
    stripe = pl.BlockSpec((seq_len, 2 * HEAD_DIM), lambda i, p: (0, i))
    return pl.pallas_call(
        attend_back_kernel,
        grid_spec=pltpu.PrefetchScalarGridSpec(
            num_scalar_prefetch=1,
            grid=(pairs,),
            in_specs=[
                queries,
                stripe,
                stripe,
                queries,
                queries,
                pl.BlockSpec((1, 8, rows), lambda i, p: (i, 0, 0)),
            ],
            out_specs=[queries, stripe, stripe],
        ),
        out_shape=[
            jax.ShapeDtypeStruct((rows, Q_WIDTH), BF),
            jax.ShapeDtypeStruct((seq_len, K_WIDTH), BF),
            jax.ShapeDtypeStruct((seq_len, K_WIDTH), BF),
        ],
        compiler_params=params(),
        cost_estimate=hint(54),
        name="attend_back",
    )(place, query, keys, values, grad, attended, log_total)


def slot_rows(positions_row, slots, rows):
    index = lax.broadcasted_iota(jnp.int32, (slots, rows), 0).astype(F32)
    return index == positions_row


def start_copies(sources, targets, sems):
    copies = [
        pltpu.make_async_copy(source, target, sems.at[k])
        for k, (source, target) in enumerate(zip(sources, targets))
    ]
    for copy in copies:
        copy.start()
    return copies


def weight_scratch(weights):
    return [pltpu.VMEM(weight.shape, BF) for weight in weights] + [
        pltpu.SemaphoreType.DMA((len(weights),))
    ]


def experts_kernel(
    sel_ref,
    own_ref,
    mate_ref,
    gate_any,
    up_any,
    down_any,
    own_part_ref,
    mate_part_ref,
    sent_ref,
    act_ref,
    row_ref,
    inner_ref,
    ret_ref,
    gate_ref,
    up_ref,
    down_ref,
    sems,
):
    copies = start_copies((gate_any, up_any, down_any), (gate_ref, up_ref, down_ref), sems)
    rows = own_ref.shape[0]
    width = gate_ref.shape[0]
    local, slots = sent_ref.shape[1:3]
    ff = down_ref.shape[1] // local
    many = 2 * slots
    combines = []
    for p, x_ref in enumerate((own_ref, mate_ref)):
        info = dot_lanes(sel_ref[...], x_ref[:, width:])
        row_ref[p] = info
        parts = []
        for e in range(local):
            hits = slot_rows(info[e : e + 1], slots, rows)
            hot = hits.astype(F32).astype(BF)
            parts.append(jnp.where(hits, info[local + e : local + e + 1], 0.0))
            for n in range(0, width, 512):
                sent_ref[p, e, :, n : n + 512] = dot(hot, x_ref[:, n : n + 512]).astype(BF)
        combines.append(jnp.concatenate(parts, axis=0).T.astype(BF))
    copies[0].wait()
    copies[1].wait()
    for e in range(local):
        sent = sent_ref[:, e].reshape(many, width)
        for f in range(0, ff, 256):
            lanes = slice(e * ff + f, e * ff + f + 256)
            gate = dot(sent, gate_ref[:, lanes])
            up = dot(sent, up_ref[:, lanes])
            act_ref[:, e, :, f : f + 256] = gate.astype(BF).reshape(2, slots, 256)
            act_ref[:, e, :, ff + f : ff + f + 256] = up.astype(BF).reshape(2, slots, 256)
            inner_ref[:, f : f + 256] = (gate / (1.0 + jnp.exp(-gate)) * up).astype(BF)
        inner = inner_ref[...]
        if e == 0:
            copies[2].wait()
        for n in range(0, width, 512):
            back = dot_lanes(inner, down_ref[n : n + 512, e * ff : (e + 1) * ff])
            ret_ref[:, e * slots : (e + 1) * slots, n : n + 512] = back.astype(BF).reshape(
                2, slots, 512
            )
    for p, part_ref in enumerate((own_part_ref, mate_part_ref)):
        for n in range(0, width, 512):
            part_ref[:, n : n + 512] = dot(combines[p], ret_ref[p, :, n : n + 512]).astype(BF)


def experts(sel, own, mate, weights, slots):
    rows = own.shape[0]
    width, all_ff = weights[2].shape
    local = EXPERTS // 8
    ff = all_ff // local
    vmem = pl.BlockSpec(memory_space=pltpu.VMEM)
    return pl.pallas_call(
        experts_kernel,
        in_specs=[vmem] * 3 + [pl.BlockSpec(memory_space=pl.ANY)] * 3,
        out_shape=[
            jax.ShapeDtypeStruct((rows, width), BF),
            jax.ShapeDtypeStruct((rows, width), BF),
            jax.ShapeDtypeStruct((2, local, slots, width), BF),
            jax.ShapeDtypeStruct((2, local, slots, 2 * ff), BF),
            jax.ShapeDtypeStruct((2, 8, rows), F32),
        ],
        scratch_shapes=[
            pltpu.VMEM((2 * slots, ff), BF),
            pltpu.VMEM((2, local * slots, width), BF),
        ]
        + weight_scratch(weights),
        compiler_params=params(),
        cost_estimate=hint(12),
        name="experts",
    )(sel, own, mate, *weights)


def experts_back_kernel(
    ids_ref,
    own_ref,
    mate_ref,
    row_ref,
    act_ref,
    gate_any,
    up_any,
    down_any,
    own_back_ref,
    mate_back_ref,
    rows_ref,
    both_ref,
    weighted_ref,
    sent_ref,
    down_ref,
    gate_ref,
    up_ref,
    sems,
):
    copies = start_copies((down_any, gate_any, up_any), (down_ref, gate_ref, up_ref), sems)
    rows, width = own_ref.shape
    local, slots = act_ref.shape[1:3]
    ff = down_ref.shape[1] // local
    many = 2 * slots
    hots = []
    for p, grad_ref in enumerate((own_ref, mate_ref)):
        parts = []
        for e in range(local):
            hot = slot_rows(row_ref[p, e : e + 1], slots, rows).astype(F32)
            parts.append(hot)
            for n in range(0, width, 512):
                rows_ref[p, e, :, n : n + 512] = dot(
                    hot.astype(BF), grad_ref[:, n : n + 512]
                ).astype(BF)
        hots.append(parts)
    copies[0].wait()
    for e in range(local):
        gates = jnp.concatenate(
            [
                jnp.sum(
                    hots[p][e] * row_ref[p, local + e : local + e + 1], axis=1, keepdims=True
                )
                for p in range(2)
            ],
            axis=0,
        )
        grad = rows_ref[:, e].reshape(many, width)
        slot_grad = jnp.zeros((many, 1), F32)
        for f in range(0, ff, 256):
            through = dot(grad, down_ref[:, e * ff + f : e * ff + f + 256])
            gate = act_ref[:, e, :, f : f + 256].reshape(many, 256).astype(F32)
            up = act_ref[:, e, :, ff + f : ff + f + 256].reshape(many, 256).astype(F32)
            sigmoid = 1.0 / (1.0 + jnp.exp(-gate))
            silu = gate * sigmoid
            inner = silu * up
            slot_grad = slot_grad + jnp.sum(inner * through, axis=1, keepdims=True)
            grad_inner = gates * through
            grad_gate = grad_inner * up * sigmoid * (1.0 + gate * (1.0 - sigmoid))
            both_ref[:, e, :, f : f + 256] = grad_gate.astype(BF).reshape(2, slots, 256)
            both_ref[:, e, :, ff + f : ff + f + 256] = (
                (grad_inner * silu).astype(BF).reshape(2, slots, 256)
            )
            weighted_ref[:, e, :, f : f + 256] = (
                (gates * inner).astype(BF).reshape(2, slots, 256)
            )
        both = both_ref[:, e].reshape(many, 2 * ff)
        if e == 0:
            copies[1].wait()
            copies[2].wait()
        lanes = slice(e * ff, (e + 1) * ff)
        for n in range(0, width, 512):
            back = dot_lanes(both[:, :ff], gate_ref[n : n + 512, lanes])
            back = back + dot_lanes(both[:, ff:], up_ref[n : n + 512, lanes])
            sent_ref[:, e * slots : (e + 1) * slots, n : n + 512] = back.astype(BF).reshape(
                2, slots, 512
            )
        high = slot_grad.astype(BF).astype(F32)
        low = slot_grad - high
        lane = lax.broadcasted_iota(jnp.int32, (many, PAD), 1)
        expert = ids_ref[e]
        extra = jnp.where(lane == expert, high, 0.0) + jnp.where(
            lane == expert + EXPERTS, low, 0.0
        )
        sent_ref[:, e * slots : (e + 1) * slots, width:] = extra.astype(BF).reshape(
            2, slots, PAD
        )
    for p, back_ref in enumerate((own_back_ref, mate_back_ref)):
        hot = jnp.concatenate(hots[p], axis=0).T.astype(BF)
        for n in range(0, width, 512):
            back_ref[:, n : n + 512] = dot(hot, sent_ref[p, :, n : n + 512]).astype(BF)
        back_ref[:, width:] = dot(hot, sent_ref[p, :, width:]).astype(BF)


def experts_back(ids, own, mate, kept, weights):
    unused, act, row_info = kept
    rows, width = own.shape
    local, slots = act.shape[1:3]
    ff = weights[2].shape[1] // local
    vmem = pl.BlockSpec(memory_space=pltpu.VMEM)
    return pl.pallas_call(
        experts_back_kernel,
        in_specs=[pl.BlockSpec(memory_space=pltpu.SMEM)]
        + [vmem] * 4
        + [pl.BlockSpec(memory_space=pl.ANY)] * 3,
        out_shape=[
            jax.ShapeDtypeStruct((rows, width + PAD), BF),
            jax.ShapeDtypeStruct((rows, width + PAD), BF),
            jax.ShapeDtypeStruct((2, local, slots, width), BF),
            jax.ShapeDtypeStruct((2, local, slots, 2 * ff), BF),
            jax.ShapeDtypeStruct((2, local, slots, ff), BF),
        ],
        scratch_shapes=[pltpu.VMEM((2, local * slots, width + PAD), BF)] + weight_scratch(weights),
        compiler_params=params(),
        cost_estimate=hint(12.5),
        name="experts_back",
    )(ids, own, mate, row_info, act, *weights)


def grads_kernel(*refs):
    count = (len(refs) - 2) // 2
    lefts, rights, out_ref, turned_ref = refs[:count], refs[count:-2], refs[-2], refs[-1]
    members, unused, slots, width = lefts[0].shape
    depth = members * slots

    @pl.when(pl.program_id(1) == 0)
    def turn_once():
        for k, left_ref in enumerate(lefts):
            for n in range(0, width, 256):
                turned_ref[n : n + 256, k * depth : (k + 1) * depth] = (
                    left_ref[:, 0, :, n : n + 256].reshape(depth, 256).T
                )

    right = jnp.concatenate(
        [right_ref[:, 0].reshape(depth, right_ref.shape[3]) for right_ref in rights], axis=0
    )

    def rows_of(index, unused):
        start = pl.multiple_of(index * 256, 256)
        out_ref[0, pl.ds(start, 256), :] = dot(turned_ref[pl.ds(start, 256), :], right).astype(BF)
        return unused

    lax.fori_loop(0, width // 256, rows_of, 0)


def expert_grads(lefts, rights):
    members, local, slots, width = lefts[0].shape
    cols = rights[0].shape[3]
    step = FF
    count = len(lefts)
    return pl.pallas_call(
        grads_kernel,
        grid=(local, cols // step),
        in_specs=[pl.BlockSpec((members, 1, slots, width), lambda e, n: (0, e, 0, 0))] * count
        + [pl.BlockSpec((members, 1, slots, step), lambda e, n: (0, e, 0, n))] * count,
        out_specs=pl.BlockSpec((1, width, step), lambda e, n: (n, 0, e)),
        out_shape=jax.ShapeDtypeStruct((cols // step, width, local * step), BF),
        scratch_shapes=[pltpu.VMEM((width, count * members * slots), BF)],
        compiler_params=params(),
        cost_estimate=hint(9 * local * cols // FF),
        name="expert_grads",
    )(*lefts, *rights)


def attention_in(hidden_in, lead, rotation, sides):
    query_full, key_value_full, unused, gain_one, unused = lead
    hat_one, factor_one = normalize(hidden_in)
    normed_one = (hat_one * gain_one[None, :]).astype(BF)
    mixed = dot(normed_one, key_value_full)
    keys_here = rotate(mixed[:, :K_WIDTH], rotation, 1.0).astype(BF)
    keys_all, values_all = sequence_gather(keys_here, mixed[:, K_WIDTH:].astype(BF), sides)
    query = dot(normed_one, query_full)
    query = rotate(query, rotation, 1.0).astype(BF) * jnp.asarray(SCALE, BF)
    return ((query, keys_all, values_all), (hat_one, factor_one, normed_one))


def attention_out(hidden_in, attended, out_full, lead, routes):
    router_full, gain_two = lead[2], lead[4]
    positions, chosen_mask, sel, ids, slots = routes
    rows = hidden_in.shape[0]
    hidden = hidden_in + dot_lanes(attended, out_full)
    hat_two, factor_two = normalize(hidden)
    normed_two = (hat_two * gain_two[None, :]).astype(BF)
    logits = dot(normed_two, router_full)
    gates = jax.nn.softmax(jnp.where(chosen_mask, logits, -jnp.inf), axis=-1)
    extra = jnp.concatenate(
        [gates.astype(BF), positions.astype(BF), jnp.zeros((rows, PAD - 2 * EXPERTS), BF)], axis=1
    )
    message = jnp.concatenate([normed_two, extra], axis=1)
    return (hidden, message, (hat_two, factor_two, normed_two, gates))


def norm_two_grad(grad_result, back, kept, lead):
    hat_two, factor_two, normed_two, gates = kept
    router_full, gain_two = lead[2], lead[4]
    width = grad_result.shape[1]
    gate_grad = back[:, width : width + EXPERTS] + back[:, width + EXPERTS : width + 2 * EXPERTS]
    grad_logits = (gates * (gate_grad - jnp.sum(gates * gate_grad, axis=-1, keepdims=True))).astype(
        BF
    )
    router_term = dot_rows(grad_logits, normed_two)
    grad_normed_two = back[:, :width] + dot_lanes(grad_logits, router_full)
    gain_two_term = jnp.sum(hat_two * grad_normed_two, axis=0)
    grad_hat_two = grad_normed_two * gain_two[None, :]
    grad_hidden = grad_result + norm_back(grad_hat_two, hat_two, factor_two)
    return (grad_hidden, router_term, gain_two_term)


def to_rows(term):
    return lax.psum_scatter(term.astype(BF), ALL_AXES, scatter_dimension=0, tiled=True)


def norm_one_grad(grad_hidden, grad_mixed, kept, lead):
    hat_one, factor_one, normed_one = kept
    query_full, key_value_full, unused, gain_one, unused = lead
    grad_normed_one = dot_lanes(grad_mixed[:, :Q_WIDTH], query_full)
    grad_normed_one = grad_normed_one + dot_lanes(grad_mixed[:, Q_WIDTH:], key_value_full)
    gain_one_term = jnp.sum(hat_one * grad_normed_one, axis=0)
    grad_hat_one = grad_normed_one * gain_one[None, :]
    return (grad_hidden + norm_back(grad_hat_one, hat_one, factor_one), gain_one_term)


FETCH0 = ("", "h0", "", "h1 x0", "h2 x1 y0")
FETCH1 = ("", "h0", "h1 x0", "", "h2 y0", "x1", "y1 x2")
DOWN1 = ("", "y0", "x0", "h0")
IN1 = ("y0", "y1 x0", "x1 h0", "", "h1")
DOWN0 = ()
IN0 = ("", "y0", "y1 x0")


def local(
    tokens,
    cotangent,
    prefix_len,
    expert_ids,
    slot_rank,
    norm1_gain,
    qkv_weight,
    out_weight,
    norm2_gain,
    router_weight,
    in_weight,
    down_weight,
):
    groups, rows, width = tokens.shape
    row_start = lax.axis_index(SEQ_AXES) * rows
    capacity = (5 * rows * TOP + 4 * EXPERTS - 1) // (4 * EXPERTS)
    slots = (capacity + 15) // 16 * 16
    positions, chosen_mask = routing(expert_ids[0], slot_rank[0, 0], capacity)
    fsdp = lax.axis_size(FSDP_AXES)
    stored = EXPERTS // fsdp
    high = lax.axis_size("fh")
    mine = []
    for high_index in range(high // 2):
        for within in range(stored):
            owner = (lax.axis_index("s0") * (high // 2) + high_index) * 4
            owner = owner + lax.axis_index("fl") * 2 + lax.axis_index("c")
            mine.append(owner * stored + within)
    ids = jnp.stack(mine).astype(jnp.int32)
    lanes = jnp.arange(PAD)[None, :]
    sel = jnp.concatenate(
        [
            (lanes == ids[:, None] + EXPERTS).astype(BF),
            (lanes == ids[:, None]).astype(BF),
            jnp.zeros((8 - 2 * len(mine), PAD), BF),
        ],
        axis=0,
    )
    routes = (positions, chosen_mask, sel, ids, slots)
    rotation = tables(row_start + jnp.arange(rows, dtype=jnp.int32))
    place = jnp.stack([prefix_len[0], row_start]).astype(jnp.int32)
    part_rows = qkv_weight.shape[1]
    weight_rows = in_weight.shape[1]

    def lead_part(index):
        return jnp.concatenate(
            [
                qkv_weight[index],
                router_weight[index],
                norm1_gain[index][:, None],
                norm2_gain[index][:, None],
                jnp.zeros((part_rows, PAD - EXPERTS - 2), BF),
            ],
            axis=1,
        )

    def gather_all(part):
        return lax.all_gather(part, ALL_AXES, axis=0, tiled=True)

    def split_lead(lead):
        wide = Q_WIDTH + 2 * K_WIDTH
        return (
            lead[:, :Q_WIDTH],
            lead[:, Q_WIDTH:wide],
            lead[:, wide : wide + EXPERTS],
            lead[:, wide + EXPERTS].astype(F32),
            lead[:, wide + EXPERTS + 1].astype(F32),
        )

    def expert_parts(index):
        part = in_weight[index]
        gates = [part[:, e * 2 * FF : e * 2 * FF + FF] for e in range(stored)]
        ups = [part[:, e * 2 * FF + FF : (e + 1) * 2 * FF] for e in range(stored)]
        return [
            jnp.concatenate(gates, axis=1),
            jnp.concatenate(ups, axis=1),
            down_weight[index],
        ]

    def forward_experts(weights):
        return lambda own, mate: experts(sel, own, mate, weights, slots)

    def backward_experts(weights, kept):
        chips = iter(kept)
        return lambda own, mate: experts_back(ids, own, mate, next(chips), weights)

    def down_grads(kept):
        return expert_grads([chip[0] for chip in kept], [chip[2] for chip in kept])[0]

    def in_grads(sents, kept):
        both = expert_grads([chip[0] for chip in sents], [chip[1] for chip in kept])
        return [both[0], both[1]]

    def follow(hops, count, plan):
        names = [name for name in hops if name != "from"]
        state = {k: hops["from"][k] for k in range(count)}
        begun = {}

        def begin(name, k):
            if (name, k) not in begun:
                begun[name, k] = hops[name][0](state[k])

        def finish(name, k, raw):
            state[k] = hops[name][1](state[k], raw)

        done = set()
        for stretch in plan:
            ends = []
            for word in stretch.split():
                name, k = word[-2], int(word[-1])
                begin(name, k)
                if word[0] != "+":
                    ends.append((name, k))
            raws = yield [begun[end] for end in ends]
            for (name, k), raw in zip(ends, raws):
                finish(name, k, raw)
                done.add((name, k))
        for name in names:
            for k in range(count):
                if (name, k) not in done:
                    begin(name, k)
                    finish(name, k, begun[name, k])
        return [state[k] for k in range(count)]

    def fetch(parts, plan):
        hops = {
            "from": parts,
            "h": (lambda part: ring_start(part, "fh"), high_end),
            "x": (lambda pair: swap(pair[1], "s0"), lambda pair, raw: low_end(pair[0], raw)),
            "y": (lambda block: ring_start(block, "s1"), rows_end),
        }
        return follow(hops, len(parts), plan)

    def deliver(terms, plan):
        hops = {
            "from": [by_rows(term) for term in terms],
            "y": (
                lambda blocks: scatter_start(blocks, "s1"),
                lambda blocks, raw: low_split(scatter_end(blocks, raw, "s1").astype(BF)),
            ),
            "x": (lambda pair: swap(pair[1], "s0"), lambda pair, raw: all_high(pair[0], raw)),
            "h": (
                lambda blocks: scatter_start(blocks, "fh"),
                lambda blocks, raw: scatter_end(blocks, raw, "fh"),
            ),
        }
        return follow(hops, len(terms), plan)

    stream = tokens.astype(F32).reshape(rows, width)
    lead0 = gather_all(lead_part(0))
    lead0, parts, out_part = tie(lead0, expert_parts(0), out_weight[0])
    fetch0 = Side(fetch(parts, FETCH0))
    out0 = lax.all_gather(out_part, FSDP_AXES, axis=0, tiled=True)
    out0 = lax.all_gather(out0, SEQ_AXES, axis=0, tiled=True)
    lead0 = split_lead(lead0)
    ready0, kept_one0 = attention_in(stream, lead0, rotation, [fetch0])
    ready0 = meet([fetch0], ready0)
    attended0, total0 = attend(*ready0, place)
    attended0 = meet([fetch0], attended0)
    hidden0, message0, kept_two0 = attention_out(stream, attended0, out0, lead0, routes)
    message0, lead_next, out_next, parts = meet(
        [fetch0], message0, lead_part(1), out_weight[1], expert_parts(1)
    )
    fetch1 = Side(fetch(parts, FETCH1))
    lead1, out1 = gather_all(lead_next), gather_all(out_next)
    weights0 = fetch0.result
    merged, kept_experts0, unused, unused = through_experts(
        message0, forward_experts(weights0), [fetch1]
    )
    stream1 = hidden0 + merged
    lead1 = split_lead(lead1)
    ready1, kept_one1 = attention_in(stream1, lead1, rotation, [fetch1])
    ready1, grad = meet([fetch1], ready1, cotangent)
    attended1, total1 = attend(*ready1, place)
    attended1 = meet([fetch1], attended1)
    hidden1, message1, kept_two1 = attention_out(stream1, attended1, out1, lead1, routes)
    message1 = meet([fetch1], message1)
    while fetch1.result is None:
        meet([fetch1])
    weights1 = fetch1.result
    forward1 = forward_experts(weights1)
    own, near, low, far, unused, unused = on_chip_pairs(message1, forward1, [])
    far = forward1(far, swap(far, "c"))
    chips1 = [own, near, low, far]
    kept_experts1 = [chip[2:] for chip in chips1]

    def attention_grad(grad_hidden, ready, attended, total, out_full, sides):
        grad_branch = grad_hidden.astype(BF)
        grad_attended = dot(grad_branch, out_full).astype(BF)
        out_term = dot_rows(grad_branch, attended).astype(BF)
        grad_attended, out_term = meet(sides, grad_attended, out_term)
        grads = attend_back(*ready, grad_attended, attended, total, place)
        share = to_rows(out_term)
        return (share, meet(sides, grads))

    def mixed_grad(grads, sides, extra):
        grad_query, grad_keys, grad_values = grads
        sums = sequence_scatter(grad_keys, grad_values)
        (key_sums, value_sums), extra = meet(sides, sums, extra)
        grad_query = rotate(grad_query.astype(F32), rotation, -1.0)
        grad_keys = rotate(rounded(key_sums), rotation, -1.0)
        return (
            jnp.concatenate([grad_query, grad_keys, value_sums], axis=-1).astype(BF),
            extra,
        )

    back1, kept, down_term, unused = through_experts(
        grad.reshape(rows, width),
        backward_experts(weights1, kept_experts1),
        [],
        late=down_grads,
    )
    back1, pairs1 = tie(back1, [chip[:2] for chip in chips1])
    output = hidden1 + chip_sums_home(*pairs1)
    grad = grad.astype(F32).reshape(rows, width)
    down_side1 = Side(deliver([down_term], DOWN1))
    grad_hidden1, router1, gain_two1 = norm_two_grad(grad, back1, kept_two1, lead1)
    out_share1, grads = attention_grad(
        grad_hidden1, ready1, attended1, total1, out1, [down_side1]
    )
    grads, kept, output = tie(grads, kept, output)
    output = output.reshape(groups, rows, width).astype(BF)
    grad_mixed1, (in_terms, out_share1) = mixed_grad(
        grads, [down_side1], (in_grads(kept_experts1, kept), out_share1)
    )
    in_side1 = Side(deliver(in_terms, IN1))
    qkv_term = dot_rows(kept_one1[2], grad_mixed1).astype(BF)
    grad, gain_one1 = norm_one_grad(grad_hidden1, grad_mixed1, kept_one1, lead1)
    grad, qkv_term = tie(grad, qkv_term)
    qkv_share1 = to_rows(qkv_term)

    side1 = [down_side1, in_side1]
    back0, kept, qkv_share1, in_terms = through_experts(
        grad.astype(BF),
        backward_experts(weights0, kept_experts0),
        side1,
        late=lambda kept: qkv_share1,
        last=lambda kept: in_grads(kept_experts0, kept),
    )
    in_side0 = Side(deliver(in_terms, IN0))
    sides = side1 + [in_side0]
    grad_hidden0, router0, gain_two0 = norm_two_grad(grad, back0, kept_two0, lead0)
    out_share0, grads = attention_grad(
        grad_hidden0, ready0, attended0, total0, out0, sides
    )
    grads, kept = tie(grads, kept)
    grad_mixed0, (out_share0, down_term) = mixed_grad(
        grads, sides, (out_share0, down_grads(kept))
    )
    down_side0 = Side(deliver([down_term], DOWN0))
    sides = sides + [down_side0]
    grad, gain_one0 = norm_one_grad(grad_hidden0, grad_mixed0, kept_one0, lead0)
    while any(side.result is None for side in sides):
        meet(sides)
    gate_share1, up_share1 = in_side1.result
    gate_share0, up_share0 = in_side0.result
    down_share1, down_share0 = down_side1.result[0], down_side0.result[0]
    gains = jnp.stack([gain_one0, gain_one1, gain_two0, gain_two1])
    smalls = jnp.concatenate(
        [router0, router1, jnp.pad(gains, ((0, PAD - 2 * EXPERTS - 4), (0, 0)))], axis=0
    ).astype(BF)
    left = jnp.concatenate([kept_one0[2], smalls], axis=0)
    right = jnp.concatenate(
        [
            jnp.pad(grad_mixed0, ((0, 0), (0, PAD))),
            jnp.pad(jnp.eye(PAD, dtype=BF), ((0, 0), (Q_WIDTH + 2 * K_WIDTH, 0))),
        ],
        axis=0,
    )
    rest = to_rows(dot_rows(left, right))
    smalls = rest[:, Q_WIDTH + 2 * K_WIDTH :].astype(F32)
    routers = jnp.stack([smalls[:, :EXPERTS], smalls[:, EXPERTS : 2 * EXPERTS]])
    gains = smalls[:, 2 * EXPERTS : 2 * EXPERTS + 4].T
    qkv_share0 = rest[:, : Q_WIDTH + 2 * K_WIDTH]

    def in_share(gate, up):
        columns = []
        for e in range(stored):
            columns += [gate[:, e * FF : (e + 1) * FF], up[:, e * FF : (e + 1) * FF]]
        return jnp.concatenate(columns, axis=1)

    return (
        output,
        grad.reshape(groups, rows, width),
        gains[:2],
        jnp.stack([qkv_share0, qkv_share1]).astype(F32),
        jnp.stack([out_share0, out_share1]).astype(F32),
        gains[2:],
        routers,
        jnp.stack([in_share(gate_share0, up_share0), in_share(gate_share1, up_share1)]),
        jnp.stack([down_share0, down_share1]),
    )


def solution(mesh):
    seq, fsdp = mesh.devices.shape
    inner_mesh = Mesh(mesh.devices.reshape(seq // 2, 2, fsdp // 4, 2, 2), ALL_AXES)
    rows = P(None, ALL_AXES)
    flat = P(None, ALL_AXES, None)
    expert = P(None, SEQ_AXES, FSDP_AXES)
    token = P(FSDP_AXES, SEQ_AXES, None)
    return jax.shard_map(
        local,
        mesh=inner_mesh,
        in_specs=(
            token,
            token,
            P(FSDP_AXES),
            token,
            token,
            rows,
            flat,
            flat,
            rows,
            flat,
            expert,
            expert,
        ),
        out_specs=(token, token, rows, flat, flat, rows, flat, expert, expert),
        check_vma=False,
    )
```

```python
import functools

import jax
import jax.numpy as jnp
from jax import lax
from jax.experimental import pallas as pl
from jax.experimental.pallas import tpu as pltpu
from jax.sharding import Mesh
from jax.sharding import PartitionSpec as P

HEADS = 24
KV_HEADS = 8
HEAD_DIM = 64
FF = 512
TOP = 8
EXPERTS = 16
LAYERS = 2
EPS = 1e-06
THETA = 10000.0
SCALE = 0.125
Q_WIDTH = HEADS * HEAD_DIM
K_WIDTH = KV_HEADS * HEAD_DIM
PAD = 128
SEQ_AXES = ("s1", "s0")
FSDP_AXES = ("fh", "fl", "c")
ALL_AXES = SEQ_AXES + FSDP_AXES
BF = jnp.bfloat16
F32 = jnp.float32


def normalize(values):
    factor = lax.rsqrt(jnp.mean(values * values, axis=-1, keepdims=True) + EPS)
    return (values * factor, factor)


def norm_back(grad_hat, hat_values, factor):
    inner = jnp.mean(grad_hat * hat_values, axis=-1, keepdims=True)
    return factor * (grad_hat - hat_values * inner)


def tables(positions):
    steps = jnp.arange(HEAD_DIM // 2, dtype=F32)
    freqs = THETA ** (-2.0 * steps / HEAD_DIM)
    angles = positions.astype(F32)[:, None] * freqs[None, :]
    cosine, sine = jnp.cos(angles), jnp.sin(angles)
    none = jnp.zeros_like(sine)
    return (
        jnp.concatenate([cosine, cosine], axis=-1),
        jnp.concatenate([-sine, none], axis=-1),
        jnp.concatenate([none, sine], axis=-1),
    )


def rotate(values, rotation, sign):
    cosine, ahead, behind = (
        jnp.tile(table, (1, values.shape[1] // HEAD_DIM)) for table in rotation
    )
    half = HEAD_DIM // 2
    later = jnp.roll(values, -half, axis=1)
    sooner = jnp.roll(values, half, axis=1)
    return values * cosine + sign * (later * ahead + sooner * behind)


def rounded(values):
    return lax.optimization_barrier(values.astype(BF)).astype(F32)


def swap(values, axis):
    return lax.ppermute(values, axis, [(0, 1), (1, 0)])


def tie(*values):
    return lax.optimization_barrier(values)


class Side:
    def __init__(self, steps):
        self.steps = steps
        self.result = None
        self.advance(None)

    def advance(self, value):
        if self.result is not None:
            return
        try:
            self.pending = self.steps.send(value)
        except StopIteration as stop:
            self.pending, self.result = (), stop.value


def meet(sides, *values):
    pending, values = tie([side.pending for side in sides], values)
    for side, value in zip(sides, pending):
        side.advance(value)
    return values[0] if len(values) == 1 else values


def ring_start(values, axis):
    size = lax.axis_size(axis)
    blocks = []
    for step in range(1, size):
        values = lax.ppermute(values, axis, [(i, (i + 1) % size) for i in range(size)])
        blocks.append(values)
    return blocks


def in_order(blocks, axis):
    size = len(blocks)
    index = lax.axis_index(axis)
    if size == 2:
        first = index == 0
        return jnp.stack(
            [jnp.where(first, blocks[0], blocks[1]), jnp.where(first, blocks[1], blocks[0])]
        )
    result = jnp.zeros((size,) + blocks[0].shape, blocks[0].dtype)
    for step, block in enumerate(blocks):
        result = lax.dynamic_update_index_in_dim(result, block, (index - step) % size, 0)
    return result


def ring_gather(values, axis):
    return in_order([values] + ring_start(values, axis), axis)


def pick(blocks, index):
    return lax.dynamic_index_in_dim(blocks, index, 0, False)


def scatter_start(blocks, axis):
    size = lax.axis_size(axis)
    index = lax.axis_index(axis)
    carried = pick(blocks, (index + size - 1) % size)
    for step in range(1, size):
        carried = lax.ppermute(carried, axis, [(i, (i + 1) % size) for i in range(size)])
        if step < size - 1:
            mine = pick(blocks, (index + size - 1 - step) % size)
            carried = (carried.astype(F32) + mine.astype(F32)).astype(BF)
    return carried


def scatter_end(blocks, carried, axis):
    return carried.astype(F32) + pick(blocks, lax.axis_index(axis)).astype(F32)


def ring_scatter(blocks, axis):
    return scatter_end(blocks, scatter_start(blocks, axis), axis)


def high_end(part, received):
    rows, cols = part.shape
    high = lax.axis_size("fh")
    low_index = lax.axis_index("s0")
    if high == 2:
        same = lax.axis_index("fh") == low_index
        return (jnp.where(same, part, received[0]), jnp.where(same, received[0], part))
    blocks = in_order([part] + received, "fh").reshape(2, high // 2, rows, cols)
    join = lambda these: these.transpose(1, 0, 2).reshape(rows, high // 2 * cols)
    return (join(pick(blocks, low_index)), join(pick(blocks, 1 - low_index)))


def low_end(keep, received):
    rows, cols = keep.shape
    return in_order([keep, received], "s0").reshape(2 * rows, cols)


def rows_end(block, received):
    return in_order([block] + received, "s1").reshape(-1, block.shape[1])


def by_rows(full):
    return full.reshape(lax.axis_size("s1"), -1, full.shape[1])


def low_split(summed):
    high = lax.axis_size("fh")
    rows = summed.shape[0] // 2
    cols = summed.shape[1] // (high // 2)
    low_index = lax.axis_index("s0")
    halves = summed.reshape(2, rows, high // 2, cols).transpose(0, 2, 1, 3)
    return (pick(halves, low_index), pick(halves, 1 - low_index))


def all_high(keep, received):
    both = in_order([keep, received], "s0")
    return both.reshape((lax.axis_size("fh"),) + keep.shape[1:])


def on_chip_pairs(message, on_chip, sides):
    half = message.shape[0] // 2
    near = swap(message, "s0")
    low = swap(message, "fl")
    own = on_chip(message, swap(message, "c"))
    near, low, own = meet(sides, near, low, own)
    far_top = swap(low[:half], "s0")
    far_bottom = swap(near[half:], "fl")
    near_mate, low_mate = tie(swap(near, "c"), swap(low, "c"))
    near, low = tie(on_chip(near, near_mate), low)
    near_sum = swap(near[1], "c")
    own_sum = swap(own[1], "c")
    low = on_chip(low, low_mate)
    far_top, far_bottom, low, near_sum, own_sum = meet(
        sides, far_top, far_bottom, low, near_sum, own_sum
    )
    far = jnp.concatenate([far_top, far_bottom], axis=0)
    return (own, near, low, far, own_sum, near_sum)


def sums_home(own, near, low, far, own_sum, near_sum, on_chip, sides, late=None, last=None):
    half = far.shape[0] // 2
    far_mate = swap(far, "c")
    low_sum = swap(low[1], "c")
    near_sum = near[0].astype(F32) + near_sum.astype(F32)
    near_top = swap(near_sum[:half].astype(BF), "s0")
    far_mate, low_sum = tie(far_mate, low_sum)
    low_sum = low[0].astype(F32) + low_sum.astype(F32)
    low_bottom = swap(low_sum[half:].astype(BF), "fl")
    far = on_chip(far, far_mate)
    near_top, low_bottom, far = tie(near_top, low_bottom, far)
    far_sum = (far[0].astype(F32) + swap(far[1], "c").astype(F32)).astype(BF)
    kept = [own[2:], near[2:], low[2:], far[2:]]
    far_top = swap(far_sum[:half], "s0")
    far_bottom = swap(far_sum[half:], "fl")
    if late is not None:
        late = late(kept)
    far_top, far_bottom, late = tie(far_top, far_bottom, late)
    near_bottom = swap((near_sum[half:] + far_bottom.astype(F32)).astype(BF), "s0")
    low_top = swap((low_sum[:half] + far_top.astype(F32)).astype(BF), "fl")
    if last is not None:
        last = last(kept)
    near_bottom, low_top, last = meet(sides, near_bottom, low_top, last)
    own_sum = own[0].astype(F32) + own_sum.astype(F32)
    top = own_sum[:half] + near_top.astype(F32) + low_top.astype(F32)
    bottom = own_sum[half:] + near_bottom.astype(F32) + low_bottom.astype(F32)
    return (jnp.concatenate([top, bottom], axis=0), kept, late, last)


def through_experts(message, on_chip, sides, late=None, last=None):
    return sums_home(
        *on_chip_pairs(message, on_chip, sides), on_chip, sides, late=late, last=last
    )


def chip_sums_home(own, near, low, far):
    half = own[0].shape[0] // 2
    own, near, low, far = (
        pair[0].astype(F32) + swap(pair[1], "c").astype(F32) for pair in (own, near, low, far)
    )
    far = far.astype(BF)
    far_top = swap(far[:half], "s0").astype(F32)
    far_bottom = swap(far[half:], "fl").astype(F32)
    near = jnp.concatenate([near[:half], near[half:] + far_bottom], axis=0).astype(BF)
    low = jnp.concatenate([low[:half] + far_top, low[half:]], axis=0).astype(BF)
    return own + swap(near, "s0").astype(F32) + swap(low, "fl").astype(F32)


def sequence_gather(keys, values, sides):
    keys_near, values_near = ring_start(keys, "s0"), ring_start(values, "s1")
    keys_near, values_near = meet(sides, keys_near, values_near)
    keys_half = in_order([keys] + keys_near, "s0")
    values_half = in_order([values] + values_near, "s1")
    keys_far, values_far = ring_start(keys_half, "s1"), ring_start(values_half, "s0")
    keys_far, values_far = meet(sides, keys_far, values_far)
    keys_all = in_order([keys_half] + keys_far, "s1")
    values_all = in_order([values_half] + values_far, "s0").transpose(1, 0, 2, 3)
    return (keys_all.reshape(-1, keys.shape[1]), values_all.reshape(-1, values.shape[1]))


def sequence_scatter(keys, values):
    outer = lax.axis_size("s1")
    width = keys.shape[1]
    keys = keys.reshape(outer, 2, -1, width)
    values = values.reshape(outer, 2, -1, width).transpose(1, 0, 2, 3)
    keys = ring_scatter(ring_scatter(keys, "s1").astype(BF), "s0")
    values = ring_scatter(ring_scatter(values, "s0").astype(BF), "s1")
    return (keys, values)


def routing(expert_ids, slot_rank, capacity):
    rows, top_count = expert_ids.shape
    pairs = expert_ids.reshape(rows * top_count)
    orders = slot_rank.reshape(rows * top_count)
    experts = jnp.arange(EXPERTS, dtype=jnp.int32)
    pair_hot = (pairs[:, None] == experts).astype(BF)
    earlier = (orders[None, :] < orders[:, None]).astype(BF)
    before = jnp.dot(earlier, pair_hot, preferred_element_type=F32)
    hot = pair_hot.astype(F32).reshape(rows, top_count, EXPERTS)
    chosen = jnp.sum(hot, axis=1)
    position = jnp.sum(before.reshape(rows, top_count, EXPERTS) * hot, axis=1)
    held = (chosen > 0.5) & (position < capacity)
    return (jnp.where(held, position, -1.0), chosen > 0.5)


VMEM_BYTES = 44 * 1024 * 1024


def params():
    return pltpu.CompilerParams(vmem_limit_bytes=VMEM_BYTES)


def hint(micros):
    flops = int(micros * 1.15e9 * 0.3)
    return pl.CostEstimate(flops=flops, bytes_accessed=1000, transcendentals=0)


def dot(left, right):
    return jnp.dot(left, right, preferred_element_type=F32)


def dot_lanes(left, right):
    return lax.dot_general(left, right, (((1,), (1,)), ((), ())), preferred_element_type=F32)


def dot_rows(left, right):
    return lax.dot_general(left, right, (((0,), (0,)), ((), ())), preferred_element_type=F32)


REPEATS = HEADS // KV_HEADS


def head_rows(block, which):
    start = which * REPEATS * HEAD_DIM
    return jnp.concatenate(
        [
            block[:, start + k * HEAD_DIM : start + (k + 1) * HEAD_DIM]
            for k in range(REPEATS)
        ],
        axis=0,
    )


def visible(block_start, rows, row_start, prefix_one, shape):
    key_pos = block_start + lax.broadcasted_iota(jnp.int32, shape, 0)
    query_pos = row_start + lax.broadcasted_iota(jnp.int32, shape, 1) % rows
    return (key_pos <= query_pos) | (key_pos < prefix_one)


def attend_kernel(place_ref, q_ref, k_ref, v_ref, o_ref, total_ref):
    rows = q_ref.shape[0]
    prefix_one, row_start = place_ref[0], place_ref[1]
    own_block = row_start // rows
    reach = jnp.maximum(row_start + rows, prefix_one)
    blocks = (reach + rows - 1) // rows
    cols = REPEATS * rows
    outs = []
    totals = []
    q_block = q_ref[...]
    for which in range(2):
        lanes = slice(which * HEAD_DIM, (which + 1) * HEAD_DIM)
        query = head_rows(q_block, which)

        def step(block, carried, masked, lanes=lanes, query=query):
            top, total, acc = carried
            start = pl.multiple_of(block * rows, rows)
            keys = k_ref[pl.ds(start, rows), lanes]
            vals = v_ref[pl.ds(start, rows), lanes]
            score = dot_lanes(keys, query)
            if masked:
                score = jnp.where(
                    visible(start, rows, row_start, prefix_one, score.shape), score, -1e30
                )
            new_top = jnp.maximum(top, jnp.max(score, axis=0, keepdims=True))
            weight = jnp.exp(score - new_top)
            shrink = jnp.exp(top - new_top)
            total = total * shrink + jnp.sum(weight, axis=0, keepdims=True)
            acc = acc * shrink + dot_rows(vals, weight.astype(BF))
            return (new_top, total, acc)

        carried = (
            jnp.full((1, cols), -1e30, F32),
            jnp.zeros((1, cols), F32),
            jnp.zeros((HEAD_DIM, cols), F32),
        )
        carried = lax.fori_loop(0, own_block, functools.partial(step, masked=False), carried)
        carried = lax.fori_loop(own_block, blocks, functools.partial(step, masked=True), carried)
        top, total, acc = carried
        result = (acc / total).T
        log_total = top + jnp.log(total)
        for k in range(REPEATS):
            outs.append(result[k * rows : (k + 1) * rows])
            totals.append(log_total[:, k * rows : (k + 1) * rows])
    o_ref[...] = jnp.concatenate(outs, axis=1).astype(BF)
    total_ref[0] = jnp.concatenate(totals + totals[:2], axis=0)


def attend(query, keys, values, place):
    rows = query.shape[0]
    seq_len = keys.shape[0]
    wide = 2 * REPEATS * HEAD_DIM
    pairs = KV_HEADS // 2
    return pl.pallas_call(
        attend_kernel,
        grid_spec=pltpu.PrefetchScalarGridSpec(
            num_scalar_prefetch=1,
            grid=(pairs,),
            in_specs=[
                pl.BlockSpec((rows, wide), lambda i, p: (0, i)),
                pl.BlockSpec((seq_len, 2 * HEAD_DIM), lambda i, p: (0, i)),
                pl.BlockSpec((seq_len, 2 * HEAD_DIM), lambda i, p: (0, i)),
            ],
            out_specs=[
                pl.BlockSpec((rows, wide), lambda i, p: (0, i)),
                pl.BlockSpec((1, 8, rows), lambda i, p: (i, 0, 0)),
            ],
        ),
        out_shape=[
            jax.ShapeDtypeStruct((rows, Q_WIDTH), BF),
            jax.ShapeDtypeStruct((pairs, 8, rows), F32),
        ],
        compiler_params=params(),
        cost_estimate=hint(36),
        name="attend",
    )(place, query, keys, values)


def attend_back_kernel(
    place_ref, q_ref, k_ref, v_ref, do_ref, o_ref, total_ref, dq_ref, dk_ref, dv_ref
):
    rows = q_ref.shape[0]
    prefix_one, row_start = place_ref[0], place_ref[1]
    own_block = row_start // rows
    reach = jnp.maximum(row_start + rows, prefix_one)
    blocks = (reach + rows - 1) // rows
    cols = REPEATS * rows
    dk_ref[...] = jnp.zeros_like(dk_ref)
    dv_ref[...] = jnp.zeros_like(dv_ref)
    q_block, do_block, o_block = q_ref[...], do_ref[...], o_ref[...]
    grads = []
    for which in range(2):
        lanes = slice(which * HEAD_DIM, (which + 1) * HEAD_DIM)
        query = head_rows(q_block, which)
        grad = head_rows(do_block, which)
        attended = head_rows(o_block, which)
        product = grad.astype(F32) * attended.astype(F32)
        delta = lax.dot_general(
            jnp.ones((8, HEAD_DIM), F32),
            product,
            (((1,), (1,)), ((), ())),
            precision=lax.Precision.HIGHEST,
            preferred_element_type=F32,
        )[:1]
        log_total = jnp.concatenate(
            [total_ref[0, which * REPEATS + k][None, :] for k in range(REPEATS)], axis=1
        )

        def step(
            block,
            acc,
            masked,
            lanes=lanes,
            query=query,
            grad=grad,
            delta=delta,
            log_total=log_total,
        ):
            start = pl.multiple_of(block * rows, rows)
            keys = k_ref[pl.ds(start, rows), lanes]
            vals = v_ref[pl.ds(start, rows), lanes]
            score = dot_lanes(keys, query)
            prob = jnp.exp(score - log_total)
            if masked:
                prob = jnp.where(
                    visible(start, rows, row_start, prefix_one, score.shape), prob, 0.0
                )
            grad_prob = dot_lanes(vals, grad)
            grad_score = (prob * (grad_prob - delta)).astype(BF)
            dv_ref[pl.ds(start, rows), lanes] = dot(prob.astype(BF), grad).astype(BF)
            dk_ref[pl.ds(start, rows), lanes] = dot(grad_score, query).astype(BF)
            return acc + dot_rows(keys, grad_score)

        acc = jnp.zeros((HEAD_DIM, cols), F32)
        acc = lax.fori_loop(0, own_block, functools.partial(step, masked=False), acc)
        acc = lax.fori_loop(own_block, blocks, functools.partial(step, masked=True), acc)
        result = (acc * SCALE).T
        for k in range(REPEATS):
            grads.append(result[k * rows : (k + 1) * rows])
    dq_ref[...] = jnp.concatenate(grads, axis=1).astype(BF)


def attend_back(query, keys, values, grad, attended, log_total, place):
    rows = query.shape[0]
    seq_len = keys.shape[0]
    wide = 2 * REPEATS * HEAD_DIM
    pairs = KV_HEADS // 2
    queries = pl.BlockSpec((rows, wide), lambda i, p: (0, i))
    stripe = pl.BlockSpec((seq_len, 2 * HEAD_DIM), lambda i, p: (0, i))
    return pl.pallas_call(
        attend_back_kernel,
        grid_spec=pltpu.PrefetchScalarGridSpec(
            num_scalar_prefetch=1,
            grid=(pairs,),
            in_specs=[
                queries,
                stripe,
                stripe,
                queries,
                queries,
                pl.BlockSpec((1, 8, rows), lambda i, p: (i, 0, 0)),
            ],
            out_specs=[queries, stripe, stripe],
        ),
        out_shape=[
            jax.ShapeDtypeStruct((rows, Q_WIDTH), BF),
            jax.ShapeDtypeStruct((seq_len, K_WIDTH), BF),
            jax.ShapeDtypeStruct((seq_len, K_WIDTH), BF),
        ],
        compiler_params=params(),
        cost_estimate=hint(54),
        name="attend_back",
    )(place, query, keys, values, grad, attended, log_total)


def slot_rows(positions_row, slots, rows):
    index = lax.broadcasted_iota(jnp.int32, (slots, rows), 0).astype(F32)
    return index == positions_row


def start_copies(sources, targets, sems):
    copies = [
        pltpu.make_async_copy(source, target, sems.at[k])
        for k, (source, target) in enumerate(zip(sources, targets))
    ]
    for copy in copies:
        copy.start()
    return copies


def weight_scratch(weights):
    return [pltpu.VMEM(weight.shape, BF) for weight in weights] + [
        pltpu.SemaphoreType.DMA((len(weights),))
    ]


def experts_kernel(
    sel_ref,
    own_ref,
    mate_ref,
    gate_any,
    up_any,
    down_any,
    own_part_ref,
    mate_part_ref,
    sent_ref,
    act_ref,
    row_ref,
    inner_ref,
    ret_ref,
    gate_ref,
    up_ref,
    down_ref,
    sems,
):
    copies = start_copies((gate_any, up_any, down_any), (gate_ref, up_ref, down_ref), sems)
    rows = own_ref.shape[0]
    width = gate_ref.shape[0]
    local, slots = sent_ref.shape[1:3]
    ff = down_ref.shape[1] // local
    many = 2 * slots
    combines = []
    for p, x_ref in enumerate((own_ref, mate_ref)):
        info = dot_lanes(sel_ref[...], x_ref[:, width:])
        row_ref[p] = info
        parts = []
        for e in range(local):
            hits = slot_rows(info[e : e + 1], slots, rows)
            hot = hits.astype(F32).astype(BF)
            parts.append(jnp.where(hits, info[local + e : local + e + 1], 0.0))
            for n in range(0, width, 512):
                sent_ref[p, e, :, n : n + 512] = dot(hot, x_ref[:, n : n + 512]).astype(BF)
        combines.append(jnp.concatenate(parts, axis=0).T.astype(BF))
    copies[0].wait()
    copies[1].wait()
    for e in range(local):
        sent = sent_ref[:, e].reshape(many, width)
        for f in range(0, ff, 256):
            lanes = slice(e * ff + f, e * ff + f + 256)
            gate = dot(sent, gate_ref[:, lanes])
            up = dot(sent, up_ref[:, lanes])
            act_ref[:, e, :, f : f + 256] = gate.astype(BF).reshape(2, slots, 256)
            act_ref[:, e, :, ff + f : ff + f + 256] = up.astype(BF).reshape(2, slots, 256)
            inner_ref[:, f : f + 256] = (gate / (1.0 + jnp.exp(-gate)) * up).astype(BF)
        inner = inner_ref[...]
        if e == 0:
            copies[2].wait()
        for n in range(0, width, 512):
            back = dot_lanes(inner, down_ref[n : n + 512, e * ff : (e + 1) * ff])
            ret_ref[:, e * slots : (e + 1) * slots, n : n + 512] = back.astype(BF).reshape(
                2, slots, 512
            )
    for p, part_ref in enumerate((own_part_ref, mate_part_ref)):
        for n in range(0, width, 512):
            part_ref[:, n : n + 512] = dot(combines[p], ret_ref[p, :, n : n + 512]).astype(BF)


def experts(sel, own, mate, weights, slots):
    rows = own.shape[0]
    width, all_ff = weights[2].shape
    local = EXPERTS // 8
    ff = all_ff // local
    vmem = pl.BlockSpec(memory_space=pltpu.VMEM)
    return pl.pallas_call(
        experts_kernel,
        in_specs=[vmem] * 3 + [pl.BlockSpec(memory_space=pl.ANY)] * 3,
        out_shape=[
            jax.ShapeDtypeStruct((rows, width), BF),
            jax.ShapeDtypeStruct((rows, width), BF),
            jax.ShapeDtypeStruct((2, local, slots, width), BF),
            jax.ShapeDtypeStruct((2, local, slots, 2 * ff), BF),
            jax.ShapeDtypeStruct((2, 8, rows), F32),
        ],
        scratch_shapes=[
            pltpu.VMEM((2 * slots, ff), BF),
            pltpu.VMEM((2, local * slots, width), BF),
        ]
        + weight_scratch(weights),
        compiler_params=params(),
        cost_estimate=hint(12),
        name="experts",
    )(sel, own, mate, *weights)


def experts_back_kernel(
    ids_ref,
    own_ref,
    mate_ref,
    row_ref,
    act_ref,
    gate_any,
    up_any,
    down_any,
    own_back_ref,
    mate_back_ref,
    rows_ref,
    both_ref,
    weighted_ref,
    sent_ref,
    down_ref,
    gate_ref,
    up_ref,
    sems,
):
    copies = start_copies((down_any, gate_any, up_any), (down_ref, gate_ref, up_ref), sems)
    rows, width = own_ref.shape
    local, slots = act_ref.shape[1:3]
    ff = down_ref.shape[1] // local
    many = 2 * slots
    hots = []
    for p, grad_ref in enumerate((own_ref, mate_ref)):
        parts = []
        for e in range(local):
            hot = slot_rows(row_ref[p, e : e + 1], slots, rows).astype(F32)
            parts.append(hot)
            for n in range(0, width, 512):
                rows_ref[p, e, :, n : n + 512] = dot(
                    hot.astype(BF), grad_ref[:, n : n + 512]
                ).astype(BF)
        hots.append(parts)
    copies[0].wait()
    for e in range(local):
        gates = jnp.concatenate(
            [
                jnp.sum(
                    hots[p][e] * row_ref[p, local + e : local + e + 1], axis=1, keepdims=True
                )
                for p in range(2)
            ],
            axis=0,
        )
        grad = rows_ref[:, e].reshape(many, width)
        slot_grad = jnp.zeros((many, 1), F32)
        for f in range(0, ff, 256):
            through = dot(grad, down_ref[:, e * ff + f : e * ff + f + 256])
            gate = act_ref[:, e, :, f : f + 256].reshape(many, 256).astype(F32)
            up = act_ref[:, e, :, ff + f : ff + f + 256].reshape(many, 256).astype(F32)
            sigmoid = 1.0 / (1.0 + jnp.exp(-gate))
            silu = gate * sigmoid
            inner = silu * up
            slot_grad = slot_grad + jnp.sum(inner * through, axis=1, keepdims=True)
            grad_inner = gates * through
            grad_gate = grad_inner * up * sigmoid * (1.0 + gate * (1.0 - sigmoid))
            both_ref[:, e, :, f : f + 256] = grad_gate.astype(BF).reshape(2, slots, 256)
            both_ref[:, e, :, ff + f : ff + f + 256] = (
                (grad_inner * silu).astype(BF).reshape(2, slots, 256)
            )
            weighted_ref[:, e, :, f : f + 256] = (
                (gates * inner).astype(BF).reshape(2, slots, 256)
            )
        both = both_ref[:, e].reshape(many, 2 * ff)
        if e == 0:
            copies[1].wait()
            copies[2].wait()
        lanes = slice(e * ff, (e + 1) * ff)
        for n in range(0, width, 512):
            back = dot_lanes(both[:, :ff], gate_ref[n : n + 512, lanes])
            back = back + dot_lanes(both[:, ff:], up_ref[n : n + 512, lanes])
            sent_ref[:, e * slots : (e + 1) * slots, n : n + 512] = back.astype(BF).reshape(
                2, slots, 512
            )
        high = slot_grad.astype(BF).astype(F32)
        low = slot_grad - high
        lane = lax.broadcasted_iota(jnp.int32, (many, PAD), 1)
        expert = ids_ref[e]
        extra = jnp.where(lane == expert, high, 0.0) + jnp.where(
            lane == expert + EXPERTS, low, 0.0
        )
        sent_ref[:, e * slots : (e + 1) * slots, width:] = extra.astype(BF).reshape(
            2, slots, PAD
        )
    for p, back_ref in enumerate((own_back_ref, mate_back_ref)):
        hot = jnp.concatenate(hots[p], axis=0).T.astype(BF)
        for n in range(0, width, 512):
            back_ref[:, n : n + 512] = dot(hot, sent_ref[p, :, n : n + 512]).astype(BF)
        back_ref[:, width:] = dot(hot, sent_ref[p, :, width:]).astype(BF)


def experts_back(ids, own, mate, kept, weights):
    unused, act, row_info = kept
    rows, width = own.shape
    local, slots = act.shape[1:3]
    ff = weights[2].shape[1] // local
    vmem = pl.BlockSpec(memory_space=pltpu.VMEM)
    return pl.pallas_call(
        experts_back_kernel,
        in_specs=[pl.BlockSpec(memory_space=pltpu.SMEM)]
        + [vmem] * 4
        + [pl.BlockSpec(memory_space=pl.ANY)] * 3,
        out_shape=[
            jax.ShapeDtypeStruct((rows, width + PAD), BF),
            jax.ShapeDtypeStruct((rows, width + PAD), BF),
            jax.ShapeDtypeStruct((2, local, slots, width), BF),
            jax.ShapeDtypeStruct((2, local, slots, 2 * ff), BF),
            jax.ShapeDtypeStruct((2, local, slots, ff), BF),
        ],
        scratch_shapes=[pltpu.VMEM((2, local * slots, width + PAD), BF)] + weight_scratch(weights),
        compiler_params=params(),
        cost_estimate=hint(12.5),
        name="experts_back",
    )(ids, own, mate, row_info, act, *weights)


def grads_kernel(*refs):
    count = (len(refs) - 2) // 2
    lefts, rights, out_ref, turned_ref = refs[:count], refs[count:-2], refs[-2], refs[-1]
    members, unused, slots, width = lefts[0].shape
    depth = members * slots

    @pl.when(pl.program_id(1) == 0)
    def turn_once():
        for k, left_ref in enumerate(lefts):
            for n in range(0, width, 256):
                turned_ref[n : n + 256, k * depth : (k + 1) * depth] = (
                    left_ref[:, 0, :, n : n + 256].reshape(depth, 256).T
                )

    right = jnp.concatenate(
        [right_ref[:, 0].reshape(depth, right_ref.shape[3]) for right_ref in rights], axis=0
    )

    def rows_of(index, unused):
        start = pl.multiple_of(index * 256, 256)
        out_ref[0, pl.ds(start, 256), :] = dot(turned_ref[pl.ds(start, 256), :], right).astype(BF)
        return unused

    lax.fori_loop(0, width // 256, rows_of, 0)


def expert_grads(lefts, rights):
    members, local, slots, width = lefts[0].shape
    cols = rights[0].shape[3]
    step = FF
    count = len(lefts)
    return pl.pallas_call(
        grads_kernel,
        grid=(local, cols // step),
        in_specs=[pl.BlockSpec((members, 1, slots, width), lambda e, n: (0, e, 0, 0))] * count
        + [pl.BlockSpec((members, 1, slots, step), lambda e, n: (0, e, 0, n))] * count,
        out_specs=pl.BlockSpec((1, width, step), lambda e, n: (n, 0, e)),
        out_shape=jax.ShapeDtypeStruct((cols // step, width, local * step), BF),
        scratch_shapes=[pltpu.VMEM((width, count * members * slots), BF)],
        compiler_params=params(),
        cost_estimate=hint(9 * local * cols // FF),
        name="expert_grads",
    )(*lefts, *rights)


def attention_in(hidden_in, lead, rotation, sides):
    query_full, key_value_full, unused, gain_one, unused = lead
    hat_one, factor_one = normalize(hidden_in)
    normed_one = (hat_one * gain_one[None, :]).astype(BF)
    mixed = dot(normed_one, key_value_full)
    keys_here = rotate(mixed[:, :K_WIDTH], rotation, 1.0).astype(BF)
    keys_all, values_all = sequence_gather(keys_here, mixed[:, K_WIDTH:].astype(BF), sides)
    query = dot(normed_one, query_full)
    query = rotate(query, rotation, 1.0).astype(BF) * jnp.asarray(SCALE, BF)
    return ((query, keys_all, values_all), (hat_one, factor_one, normed_one))


def attention_out(hidden_in, attended, out_full, lead, routes):
    router_full, gain_two = lead[2], lead[4]
    positions, chosen_mask, sel, ids, slots = routes
    rows = hidden_in.shape[0]
    hidden = hidden_in + dot_lanes(attended, out_full)
    hat_two, factor_two = normalize(hidden)
    normed_two = (hat_two * gain_two[None, :]).astype(BF)
    logits = dot(normed_two, router_full)
    gates = jax.nn.softmax(jnp.where(chosen_mask, logits, -jnp.inf), axis=-1)
    extra = jnp.concatenate(
        [gates.astype(BF), positions.astype(BF), jnp.zeros((rows, PAD - 2 * EXPERTS), BF)], axis=1
    )
    message = jnp.concatenate([normed_two, extra], axis=1)
    return (hidden, message, (hat_two, factor_two, normed_two, gates))


def norm_two_grad(grad_result, back, kept, lead):
    hat_two, factor_two, normed_two, gates = kept
    router_full, gain_two = lead[2], lead[4]
    width = grad_result.shape[1]
    gate_grad = back[:, width : width + EXPERTS] + back[:, width + EXPERTS : width + 2 * EXPERTS]
    grad_logits = (gates * (gate_grad - jnp.sum(gates * gate_grad, axis=-1, keepdims=True))).astype(
        BF
    )
    router_term = dot_rows(grad_logits, normed_two)
    grad_normed_two = back[:, :width] + dot_lanes(grad_logits, router_full)
    gain_two_term = jnp.sum(hat_two * grad_normed_two, axis=0)
    grad_hat_two = grad_normed_two * gain_two[None, :]
    grad_hidden = grad_result + norm_back(grad_hat_two, hat_two, factor_two)
    return (grad_hidden, router_term, gain_two_term)


def to_rows(term):
    return lax.psum_scatter(term.astype(BF), ALL_AXES, scatter_dimension=0, tiled=True)


def norm_one_grad(grad_hidden, grad_mixed, kept, lead):
    hat_one, factor_one, normed_one = kept
    query_full, key_value_full, unused, gain_one, unused = lead
    grad_normed_one = dot_lanes(grad_mixed[:, :Q_WIDTH], query_full)
    grad_normed_one = grad_normed_one + dot_lanes(grad_mixed[:, Q_WIDTH:], key_value_full)
    gain_one_term = jnp.sum(hat_one * grad_normed_one, axis=0)
    grad_hat_one = grad_normed_one * gain_one[None, :]
    return (grad_hidden + norm_back(grad_hat_one, hat_one, factor_one), gain_one_term)


FETCH0 = ("", "h0", "", "h1 x0", "h2 x1 y0")
FETCH1 = ("", "h0", "h1 x0", "", "h2 y0", "x1", "y1 x2")
DOWN1 = ("", "y0", "x0", "h0")
IN1 = ("y0", "y1 x0", "x1 h0", "", "h1")
DOWN0 = ()
IN0 = ("", "y0 y1", "x0")


def local(
    tokens,
    cotangent,
    prefix_len,
    expert_ids,
    slot_rank,
    norm1_gain,
    qkv_weight,
    out_weight,
    norm2_gain,
    router_weight,
    in_weight,
    down_weight,
):
    groups, rows, width = tokens.shape
    row_start = lax.axis_index(SEQ_AXES) * rows
    capacity = (5 * rows * TOP + 4 * EXPERTS - 1) // (4 * EXPERTS)
    slots = (capacity + 15) // 16 * 16
    positions, chosen_mask = routing(expert_ids[0], slot_rank[0, 0], capacity)
    fsdp = lax.axis_size(FSDP_AXES)
    stored = EXPERTS // fsdp
    high = lax.axis_size("fh")
    mine = []
    for high_index in range(high // 2):
        for within in range(stored):
            owner = (lax.axis_index("s0") * (high // 2) + high_index) * 4
            owner = owner + lax.axis_index("fl") * 2 + lax.axis_index("c")
            mine.append(owner * stored + within)
    ids = jnp.stack(mine).astype(jnp.int32)
    lanes = jnp.arange(PAD)[None, :]
    sel = jnp.concatenate(
        [
            (lanes == ids[:, None] + EXPERTS).astype(BF),
            (lanes == ids[:, None]).astype(BF),
            jnp.zeros((8 - 2 * len(mine), PAD), BF),
        ],
        axis=0,
    )
    routes = (positions, chosen_mask, sel, ids, slots)
    rotation = tables(row_start + jnp.arange(rows, dtype=jnp.int32))
    place = jnp.stack([prefix_len[0], row_start]).astype(jnp.int32)
    part_rows = qkv_weight.shape[1]
    weight_rows = in_weight.shape[1]

    def lead_part(index):
        return jnp.concatenate(
            [
                qkv_weight[index],
                router_weight[index],
                norm1_gain[index][:, None],
                norm2_gain[index][:, None],
                jnp.zeros((part_rows, PAD - EXPERTS - 2), BF),
            ],
            axis=1,
        )

    def gather_all(part):
        return lax.all_gather(part, ALL_AXES, axis=0, tiled=True)

    def split_lead(lead):
        wide = Q_WIDTH + 2 * K_WIDTH
        return (
            lead[:, :Q_WIDTH],
            lead[:, Q_WIDTH:wide],
            lead[:, wide : wide + EXPERTS],
            lead[:, wide + EXPERTS].astype(F32),
            lead[:, wide + EXPERTS + 1].astype(F32),
        )

    def expert_parts(index):
        part = in_weight[index]
        gates = [part[:, e * 2 * FF : e * 2 * FF + FF] for e in range(stored)]
        ups = [part[:, e * 2 * FF + FF : (e + 1) * 2 * FF] for e in range(stored)]
        return [
            jnp.concatenate(gates, axis=1),
            jnp.concatenate(ups, axis=1),
            down_weight[index],
        ]

    def forward_experts(weights):
        return lambda own, mate: experts(sel, own, mate, weights, slots)

    def backward_experts(weights, kept):
        chips = iter(kept)
        return lambda own, mate: experts_back(ids, own, mate, next(chips), weights)

    def down_grads(kept):
        return expert_grads([chip[0] for chip in kept], [chip[2] for chip in kept])[0]

    def in_grads(sents, kept):
        both = expert_grads([chip[0] for chip in sents], [chip[1] for chip in kept])
        return [both[0], both[1]]

    def follow(hops, count, plan):
        names = [name for name in hops if name != "from"]
        state = {k: hops["from"][k] for k in range(count)}
        begun = {}

        def begin(name, k):
            if (name, k) not in begun:
                begun[name, k] = hops[name][0](state[k])

        def finish(name, k, raw):
            state[k] = hops[name][1](state[k], raw)

        done = set()
        for stretch in plan:
            ends = []
            for word in stretch.split():
                name, k = word[-2], int(word[-1])
                begin(name, k)
                if word[0] != "+":
                    ends.append((name, k))
            raws = yield [begun[end] for end in ends]
            for (name, k), raw in zip(ends, raws):
                finish(name, k, raw)
                done.add((name, k))
        for name in names:
            for k in range(count):
                if (name, k) not in done:
                    begin(name, k)
                    finish(name, k, begun[name, k])
        return [state[k] for k in range(count)]

    def fetch(parts, plan):
        hops = {
            "from": parts,
            "h": (lambda part: ring_start(part, "fh"), high_end),
            "x": (lambda pair: swap(pair[1], "s0"), lambda pair, raw: low_end(pair[0], raw)),
            "y": (lambda block: ring_start(block, "s1"), rows_end),
        }
        return follow(hops, len(parts), plan)

    def deliver(terms, plan):
        hops = {
            "from": [by_rows(term) for term in terms],
            "y": (
                lambda blocks: scatter_start(blocks, "s1"),
                lambda blocks, raw: low_split(scatter_end(blocks, raw, "s1").astype(BF)),
            ),
            "x": (lambda pair: swap(pair[1], "s0"), lambda pair, raw: all_high(pair[0], raw)),
            "h": (
                lambda blocks: scatter_start(blocks, "fh"),
                lambda blocks, raw: scatter_end(blocks, raw, "fh"),
            ),
        }
        return follow(hops, len(terms), plan)

    stream = tokens.astype(F32).reshape(rows, width)
    lead0 = gather_all(lead_part(0))
    lead0, parts, out_part = tie(lead0, expert_parts(0), out_weight[0])
    fetch0 = Side(fetch(parts, FETCH0))
    out0 = lax.all_gather(out_part, FSDP_AXES, axis=0, tiled=True)
    out0 = lax.all_gather(out0, SEQ_AXES, axis=0, tiled=True)
    lead0 = split_lead(lead0)
    ready0, kept_one0 = attention_in(stream, lead0, rotation, [fetch0])
    ready0 = meet([fetch0], ready0)
    attended0, total0 = attend(*ready0, place)
    attended0 = meet([fetch0], attended0)
    hidden0, message0, kept_two0 = attention_out(stream, attended0, out0, lead0, routes)
    message0, lead_next, out_next, parts = meet(
        [fetch0], message0, lead_part(1), out_weight[1], expert_parts(1)
    )
    fetch1 = Side(fetch(parts, FETCH1))
    lead1, out1 = gather_all(lead_next), gather_all(out_next)
    weights0 = fetch0.result
    merged, kept_experts0, unused, unused = through_experts(
        message0, forward_experts(weights0), [fetch1]
    )
    stream1 = hidden0 + merged
    lead1 = split_lead(lead1)
    ready1, kept_one1 = attention_in(stream1, lead1, rotation, [fetch1])
    ready1, grad = meet([fetch1], ready1, cotangent)
    attended1, total1 = attend(*ready1, place)
    attended1 = meet([fetch1], attended1)
    hidden1, message1, kept_two1 = attention_out(stream1, attended1, out1, lead1, routes)
    message1 = meet([fetch1], message1)
    while fetch1.result is None:
        meet([fetch1])
    weights1 = fetch1.result
    forward1 = forward_experts(weights1)
    own, near, low, far, unused, unused = on_chip_pairs(message1, forward1, [])
    far = forward1(far, swap(far, "c"))
    chips1 = [own, near, low, far]
    kept_experts1 = [chip[2:] for chip in chips1]

    def attention_grad(grad_hidden, ready, attended, total, out_full, sides):
        grad_branch = grad_hidden.astype(BF)
        grad_attended = dot(grad_branch, out_full).astype(BF)
        out_term = dot_rows(grad_branch, attended).astype(BF)
        grad_attended, out_term = meet(sides, grad_attended, out_term)
        grads = attend_back(*ready, grad_attended, attended, total, place)
        share = to_rows(out_term)
        return (share, meet(sides, grads))

    def mixed_grad(grads, sides, extra):
        grad_query, grad_keys, grad_values = grads
        sums = sequence_scatter(grad_keys, grad_values)
        (key_sums, value_sums), extra = meet(sides, sums, extra)
        grad_query = rotate(grad_query.astype(F32), rotation, -1.0)
        grad_keys = rotate(rounded(key_sums), rotation, -1.0)
        return (
            jnp.concatenate([grad_query, grad_keys, value_sums], axis=-1).astype(BF),
            extra,
        )

    back1, kept, down_term, unused = through_experts(
        grad.reshape(rows, width),
        backward_experts(weights1, kept_experts1),
        [],
        late=down_grads,
    )
    back1, pairs1 = tie(back1, [chip[:2] for chip in chips1])
    output = hidden1 + chip_sums_home(*pairs1)
    grad = grad.astype(F32).reshape(rows, width)
    down_side1 = Side(deliver([down_term], DOWN1))
    grad_hidden1, router1, gain_two1 = norm_two_grad(grad, back1, kept_two1, lead1)
    out_share1, grads = attention_grad(
        grad_hidden1, ready1, attended1, total1, out1, [down_side1]
    )
    grads, kept, output = tie(grads, kept, output)
    output = output.reshape(groups, rows, width).astype(BF)
    grad_mixed1, (in_terms, out_share1) = mixed_grad(
        grads, [down_side1], (in_grads(kept_experts1, kept), out_share1)
    )
    in_side1 = Side(deliver(in_terms, IN1))
    qkv_term = dot_rows(kept_one1[2], grad_mixed1).astype(BF)
    grad, gain_one1 = norm_one_grad(grad_hidden1, grad_mixed1, kept_one1, lead1)
    grad, qkv_term = tie(grad, qkv_term)
    qkv_share1 = to_rows(qkv_term)

    side1 = [down_side1, in_side1]
    back0, kept, qkv_share1, in_terms = through_experts(
        grad.astype(BF),
        backward_experts(weights0, kept_experts0),
        side1,
        late=lambda kept: qkv_share1,
        last=lambda kept: in_grads(kept_experts0, kept),
    )
    in_side0 = Side(deliver(in_terms, IN0))
    sides = side1 + [in_side0]
    grad_hidden0, router0, gain_two0 = norm_two_grad(grad, back0, kept_two0, lead0)
    out_share0, grads = attention_grad(
        grad_hidden0, ready0, attended0, total0, out0, sides
    )
    grads, kept = tie(grads, kept)
    grad_mixed0, (out_share0, down_term) = mixed_grad(
        grads, sides, (out_share0, down_grads(kept))
    )
    down_side0 = Side(deliver([down_term], DOWN0))
    sides = sides + [down_side0]
    grad, gain_one0 = norm_one_grad(grad_hidden0, grad_mixed0, kept_one0, lead0)
    while any(side.result is None for side in sides):
        meet(sides)
    gate_share1, up_share1 = in_side1.result
    gate_share0, up_share0 = in_side0.result
    down_share1, down_share0 = down_side1.result[0], down_side0.result[0]
    gains = jnp.stack([gain_one0, gain_one1, gain_two0, gain_two1])
    smalls = jnp.concatenate(
        [router0, router1, jnp.pad(gains, ((0, PAD - 2 * EXPERTS - 4), (0, 0)))], axis=0
    ).astype(BF)
    left = jnp.concatenate([kept_one0[2], smalls], axis=0)
    right = jnp.concatenate(
        [
            jnp.pad(grad_mixed0, ((0, 0), (0, PAD))),
            jnp.pad(jnp.eye(PAD, dtype=BF), ((0, 0), (Q_WIDTH + 2 * K_WIDTH, 0))),
        ],
        axis=0,
    )
    rest = to_rows(dot_rows(left, right))
    smalls = rest[:, Q_WIDTH + 2 * K_WIDTH :].astype(F32)
    routers = jnp.stack([smalls[:, :EXPERTS], smalls[:, EXPERTS : 2 * EXPERTS]])
    gains = smalls[:, 2 * EXPERTS : 2 * EXPERTS + 4].T
    qkv_share0 = rest[:, : Q_WIDTH + 2 * K_WIDTH]

    def in_share(gate, up):
        columns = []
        for e in range(stored):
            columns += [gate[:, e * FF : (e + 1) * FF], up[:, e * FF : (e + 1) * FF]]
        return jnp.concatenate(columns, axis=1)

    return (
        output,
        grad.reshape(groups, rows, width),
        gains[:2],
        jnp.stack([qkv_share0, qkv_share1]).astype(F32),
        jnp.stack([out_share0, out_share1]).astype(F32),
        gains[2:],
        routers,
        jnp.stack([in_share(gate_share0, up_share0), in_share(gate_share1, up_share1)]),
        jnp.stack([down_share0, down_share1]),
    )


def solution(mesh):
    seq, fsdp = mesh.devices.shape
    inner_mesh = Mesh(mesh.devices.reshape(seq // 2, 2, fsdp // 4, 2, 2), ALL_AXES)
    rows = P(None, ALL_AXES)
    flat = P(None, ALL_AXES, None)
    expert = P(None, SEQ_AXES, FSDP_AXES)
    token = P(FSDP_AXES, SEQ_AXES, None)
    return jax.shard_map(
        local,
        mesh=inner_mesh,
        in_specs=(
            token,
            token,
            P(FSDP_AXES),
            token,
            token,
            rows,
            flat,
            flat,
            rows,
            flat,
            expert,
            expert,
        ),
        out_specs=(token, token, rows, flat, flat, rows, flat, expert, expert),
        check_vma=False,
    )
```
